32 devices in a mesh: grp: 4 (over x, core), ang: 8 (over z, y).
Axes of the slice: x: 2, y: 2, z: 4, core: 2. Of those that a mesh axis runs over, the one named last changes fastest.
Arguments:
- current: bfloat16 [2, 4096, 256], P(None, ('grp', 'ang')), may hold values from -6 to 6
- near_blocks: bfloat16 [1280, 2, 256, 256], P(('grp', 'ang')), may hold values from -0.25 to 0.25
- near_rows: int32 [1280], P(('grp', 'ang')), may hold values from 0 to 127
- near_cols: int32 [1280], P(('grp', 'ang')), may hold values from 0 to 1023
- radiate: float32 [2, 1024, 256], replicated, may hold values from -0.25 to 0.25
- receive: float32 [2, 1024, 256], replicated, may hold values from -0.109375 to 0.109375
- interp: float32 [1536, 1024], replicated, may hold values from -0.1875 to 0.1875
- shift_phase: float32 [8, 1536], replicated, may hold values from -3.140625 to 3.140625
- translate: float32 [2, 316, 1536], P(None, None, 'ang'), may hold values from -0.375 to 0.375
- far_sources: int32 [512, 16], P('grp'), may hold values from 0 to 511
- far_types: int32 [512, 16], P('grp'), may hold values from 0 to 315
Outputs:
- product: float32 [2, 4096, 256], P(None, ('grp', 'ang'))
The draws below stay inside these ranges and needn't reach their ends.
Inputs may be any that keep to these rules, and one draw needn't show every extreme that they name: Block b is stored on device b div 40; near_rows[b] is one of that device's own 128 clusters. near_cols[b] is one of the 1024 clusters of block b's grp index, counted from that group's first cluster. `far_sources`: parent p holds leaf clusters 8 p to 8 p + 7; entries are global parent numbers. `far_types`: an index into the second dimension of translate.
All inputs are finite; a program needn't handle non-finite values.
Results may differ from the reference program's by a relative error of at most 0.0003.
Values may be sent and summed in bfloat16 or wider, within the bound.
No kernel may reach another device: no remote copies, remote signals or barrier semaphores. Data moves between devices by JAX's collectives and lax.ppermute only.
A program may use at most 128 MiB of HBM per device.

```python
import math
import jax
import jax.numpy as jnp
import numpy as np
from jax import lax

UNK = 256
K_LEAF = 1024
K_UP = 1536
NT = 316
M_LIST = 16
CL_DEV = 128
NB_DEV = 40
CLUST = 4096
PTOT = 512
NBLK = 1280
N_GRP = 4
N_ANG = 8


def touch_ends(entries, stream_key, smallest, high):
    shape = entries.shape
    index_at = [jax.random.randint(jax.random.fold_in(stream_key, axis), (), 0, shape[axis]) for axis in range(len(shape))]
    entries = entries.at[tuple(index_at)].set(smallest)
    longest = shape.index(max(shape))
    index_at[longest] = (index_at[longest] + 1) % shape[longest]
    return entries.at[tuple(index_at)].set(high)


def level_of(stream_key, extent, shards, low, largest):
    def one(axis_at, blocks):
        heights = jax.random.uniform(jax.random.fold_in(jax.random.fold_in(stream_key, 6), axis_at), (blocks,), jnp.float32, low / len(shards), largest / len(shards))
        return jnp.repeat(jnp.exp(heights), extent[axis_at] // blocks).reshape((-1,) + (1,) * (len(extent) - axis_at - 1))

    loudness = one(*shards[0])
    for cut in shards[1:]:
        loudness = loudness * one(*cut)
    return loudness


def rank_table(amount, lean):
    weights = [(1 << 20) // math.isqrt(standing ** lean) + 1 for standing in range(1, amount + 1)]
    scale = 1 + sum(weights) // (1 << 30)
    return np.cumsum(np.array([max(1, weight // scale) for weight in weights]))


def ranked_ids(key, shape, count, skew):
    table = rank_table(count, skew)
    lot = jax.random.randint(jax.random.fold_in(key, 1), shape, 0, int(table[count - 1]))
    rank = jnp.searchsorted(jnp.asarray(table, jnp.int32), lot, side="right")
    return jax.random.permutation(jax.random.fold_in(key, 2), count)[rank].astype(jnp.int32)


def gaussian(own_key, shape, scale, bound, cuts=(), held_as=jnp.bfloat16):
    array = jax.random.normal(own_key, shape, jnp.float32) * scale
    if len(cuts) > 0:
        array = level_of(own_key, shape, cuts, -0.22, 0.18) * array
    return jnp.clip(array, min=-bound, max=bound).astype(held_as)


def setup_inputs(seed: int = 0) -> dict:
    seeds = jax.random.split(jax.random.key(seed), 12)
    current = gaussian(seeds[0], (2, CLUST, UNK), 1.0, 6.0, ((1, 32),))
    near_blocks = gaussian(seeds[1], (NBLK, 2, UNK, UNK), (2 * UNK) ** -0.5, 0.25, ((0, 32),))
    near_rows = touch_ends(ranked_ids(seeds[2], (NBLK,), CL_DEV, 2), jax.random.fold_in(seeds[2], 3), 0, CL_DEV - 1).astype(jnp.int32)
    near_cols = touch_ends(jax.random.randint(seeds[3], (NBLK,), 0, CL_DEV * N_ANG), jax.random.fold_in(seeds[3], 1), 0, (CL_DEV * N_ANG) - 1).astype(jnp.int32)
    radiate = gaussian(seeds[4], (2, K_LEAF, UNK), (2 * UNK) ** -0.5, 0.25, (), jnp.float32)
    receive = gaussian(seeds[5], (2, K_LEAF, UNK), (3 * K_LEAF) ** -0.5, 0.109375, (), jnp.float32)
    interp = gaussian(seeds[6], (K_UP, K_LEAF), K_LEAF ** -0.5, 0.1875, (), jnp.float32)
    shift_phase = jnp.clip(jax.random.uniform(seeds[7], (8, K_UP), jnp.float32, -3.140625, 3.140625), -3.140625, 3.140625)
    translate = gaussian(seeds[8], (2, NT, K_UP), (16 * M_LIST) ** -0.5, 0.375, ((2, 8),), jnp.float32)
    far_sources = touch_ends(jax.random.randint(seeds[9], (PTOT, M_LIST), 0, PTOT), jax.random.fold_in(seeds[9], 1), 0, PTOT - 1).astype(jnp.int32)
    far_types = touch_ends(jax.random.randint(seeds[10], (PTOT, M_LIST), 0, NT), jax.random.fold_in(seeds[10], 1), 0, NT - 1).astype(jnp.int32)
    return dict(current=current, near_blocks=near_blocks, near_rows=near_rows, near_cols=near_cols, radiate=radiate, receive=receive, interp=interp, shift_phase=shift_phase, translate=translate, far_sources=far_sources, far_types=far_types)


HIGHEST = lax.Precision.HIGHEST


def complex_product(formula, left_side, right_side):
    real_part = jnp.einsum(formula, left_side[0], right_side[0], precision=HIGHEST) - jnp.einsum(formula, left_side[1], right_side[1], precision=HIGHEST)
    imag_part = jnp.einsum(formula, left_side[0], right_side[1], precision=HIGHEST) + jnp.einsum(formula, left_side[1], right_side[0], precision=HIGHEST)
    return jnp.stack([real_part, imag_part])


def shift_sum(children, cosine, sine_part):
    grouped = children.reshape(2, children.shape[1], children.shape[2] // 8, 8)
    cos_t = cosine.T[:, None, :]
    sin_t = sine_part.T[:, None, :]
    real_part = jnp.sum(cos_t * grouped[0] - sin_t * grouped[1], axis=2)
    imag_part = jnp.sum(cos_t * grouped[1] + sin_t * grouped[0], axis=2)
    return jnp.stack([real_part, imag_part])


def spread(parents, cosine, sine_part):
    cos_t = cosine.T[:, None, :]
    sin_t = sine_part.T[:, None, :]
    par_real = parents[0][:, :, None]
    par_imag = parents[1][:, :, None]
    real_part = cos_t * par_real + sin_t * par_imag
    imag_part = cos_t * par_imag - sin_t * par_real
    width = parents.shape[2] * 8
    return jnp.stack([real_part.reshape(parents.shape[1], width), imag_part.reshape(parents.shape[1], width)])


def reference(current, near_blocks, near_rows, near_cols, radiate, receive, interp, shift_phase, translate, far_sources, far_types):
    as_float = current.astype(jnp.float32)
    cosine = jnp.cos(shift_phase)
    sine_part = jnp.sin(shift_phase)
    radiated = complex_product("kn,cn->kc", radiate, as_float)
    children = jnp.einsum("jk,skc->sjc", interp, radiated, precision=HIGHEST)
    parents = shift_sum(children, cosine, sine_part)

    def add_entry(slot_index, total):
        chosen = jnp.take(parents, far_sources[:, slot_index], axis=2)
        factor = jnp.transpose(jnp.take(translate, far_types[:, slot_index], axis=1), (0, 2, 1))
        real_part = factor[0] * chosen[0] - factor[1] * chosen[1]
        imag_part = factor[0] * chosen[1] + factor[1] * chosen[0]
        return total + jnp.stack([real_part, imag_part])

    incoming = lax.fori_loop(0, M_LIST, add_entry, jnp.zeros(parents.shape, jnp.float32))
    child_in = spread(incoming, cosine, sine_part)
    leaf_in = jnp.einsum("jk,sjc->skc", interp, child_in, precision=HIGHEST)
    far_part = complex_product("kn,kc->cn", receive, leaf_in)

    device_count = N_GRP * N_ANG
    block_ids = jnp.arange(NB_DEV * device_count, dtype=jnp.int32)
    owners = block_ids // NB_DEV
    rows_global = (owners * CL_DEV + near_rows).astype(jnp.int32)
    cols_global = ((owners // N_ANG) * (CL_DEV * N_ANG) + near_cols).astype(jnp.int32)

    def per_device(device_index):
        first_block = (device_index * NB_DEV).astype(jnp.int32)
        block_group = lax.dynamic_slice_in_dim(near_blocks, first_block, NB_DEV, 0).astype(jnp.float32)
        col_ids = lax.dynamic_slice_in_dim(cols_global, first_block, NB_DEV, 0)
        picked = jnp.take(as_float, col_ids, axis=1)
        real_part = jnp.einsum("bmn,bn->bm", block_group[:, 0], picked[0]) - jnp.einsum("bmn,bn->bm", block_group[:, 1], picked[1])
        imag_part = jnp.einsum("bmn,bn->bm", block_group[:, 0], picked[1]) + jnp.einsum("bmn,bn->bm", block_group[:, 1], picked[0])
        return jnp.stack([real_part, imag_part], axis=1)

    contrib = lax.map(per_device, jnp.arange(device_count, dtype=jnp.int32))
    contrib = contrib.reshape(NB_DEV * device_count, 2, UNK)
    near_part = jax.ops.segment_sum(contrib, rows_global, num_segments=CL_DEV * device_count)
    near_part = jnp.transpose(near_part, (1, 0, 2))
    return far_part + near_part
```

```python
import functools
import jax
import jax.numpy as jnp
from jax import lax
from jax.experimental import pallas as pl
from jax.experimental.pallas import tpu as pltpu
from jax.sharding import PartitionSpec as P

F32 = jnp.float32
BF16 = jnp.bfloat16
VMEM_LIMIT = 48 << 20


def halves(x):
    high = x.astype(BF16)
    return high, (x - high.astype(F32)).astype(BF16)


def dot_nt(a, b):
    return lax.dot_general(a, b, (((1,), (1,)), ((), ())), preferred_element_type=F32)


def dot_nn(a, b):
    return lax.dot_general(a, b, (((1,), (0,)), ((), ())), preferred_element_type=F32)


def iota(shape, dim):
    return lax.broadcasted_iota(jnp.int32, shape, dim)


class Layout:
    def __init__(self, n_grp, n_ang, k_up, list_len):
        self.n_grp, self.n_ang = n_grp, n_ang
        self.n_dev = n_grp * n_ang
        self.own = k_up // self.n_dev
        self.pad = -(-self.own // 8) * 8
        self.lists = 2 * self.pad
        self.list_len = list_len

    def first(self, dest):
        grp, ang = divmod(dest, self.n_ang)
        return (ang * self.n_grp + grp) * self.own


def forward_kernel(lay, cur_ref, rad_ref, interp_ref, cos_ref, sin_ref, lists_ref, out_ref,
                   high_ref, low_ref, par_ref):
    step = pl.program_id(0)
    count = cur_ref.shape[1]
    n_par = count // 8

    @pl.when(step == 0)
    def _():
        row = iota((count, count), 0)
        col = iota((count, count), 1)
        order = (col == (row % n_par) * 8 + row // n_par).astype(BF16)
        cur_re = dot_nn(order, cur_ref[0]).astype(BF16)
        cur_im = dot_nn(order, cur_ref[1]).astype(BF16)
        left = jnp.concatenate([cur_re, cur_im], axis=0)
        right = jnp.concatenate([-cur_im, cur_re], axis=0)
        k_leaf = rad_ref.shape[1]
        width = 256
        for k in range(0, k_leaf, width):
            rr_high, rr_low = halves(rad_ref[0, k:k + width, :])
            ri_high, ri_low = halves(rad_ref[1, k:k + width, :])
            radiated = (dot_nt(left, rr_high) + dot_nt(left, rr_low)
                        + dot_nt(right, ri_high) + dot_nt(right, ri_low))
            high, low = halves(radiated)
            high_ref[:, k:k + width] = high
            low_ref[:, k:k + width] = low

    in_high, in_low = halves(interp_ref[...])
    children = dot_nt(high_ref[...], in_high) + dot_nt(high_ref[...], in_low) + dot_nt(low_ref[...], in_high)
    re_sum = im_sum = None
    for t in range(8):
        c = cos_ref[t:t + 1, :]
        s = sin_ref[t:t + 1, :]
        re = children[t * n_par:(t + 1) * n_par]
        im = children[count + t * n_par:count + (t + 1) * n_par]
        re_t = c * re - s * im
        im_t = c * im + s * re
        re_sum = re_t if t == 0 else re_sum + re_t
        im_sum = im_t if t == 0 else im_sum + im_t
    width = interp_ref.shape[0]
    at = pl.ds(pl.multiple_of(step * width, width), width)
    par_ref[0, :, at] = re_sum
    par_ref[1, :, at] = im_sum

    @pl.when(step == pl.num_programs(0) - 1)
    def _():
        out_ref[...] = jnp.zeros_like(out_ref)
        for dest in range(lay.n_dev):
            j = lay.first(dest)
            out_ref[dest, :, 0:lay.own] = par_ref[0, :, j:j + lay.own]
            out_ref[dest, :, lay.pad:lay.pad + lay.own] = par_ref[1, :, j:j + lay.own]
            out_ref[dest, :, lay.lists:lay.lists + lay.list_len] = lists_ref[...]


def forward(lay, current, radiate, interp, cosine, sine, lists):
    count, unk = current.shape[1:]
    k_leaf = radiate.shape[1]
    k_up = interp.shape[0]
    width = 256
    n_par = count // 8
    whole = lambda *shape: pl.BlockSpec(shape, lambda i: (0,) * len(shape))
    return pl.pallas_call(
        functools.partial(forward_kernel, lay),
        grid=(k_up // width,),
        in_specs=[
            whole(2, count, unk),
            whole(2, k_leaf, unk),
            pl.BlockSpec((width, k_leaf), lambda i: (i, 0)),
            pl.BlockSpec((8, width), lambda i: (0, i)),
            pl.BlockSpec((8, width), lambda i: (0, i)),
            whole(n_par, lay.list_len),
        ],
        out_specs=whole(lay.n_dev, n_par, 128),
        out_shape=jax.ShapeDtypeStruct((lay.n_dev, n_par, 128), F32),
        scratch_shapes=[
            pltpu.VMEM((2 * count, k_leaf), BF16),
            pltpu.VMEM((2 * count, k_leaf), BF16),
            pltpu.VMEM((2, n_par, k_up), F32),
        ],
        compiler_params=pltpu.CompilerParams(vmem_limit_bytes=VMEM_LIMIT),
        cost_estimate=pl.CostEstimate(flops=3 * 10**9, bytes_accessed=9 * 10**6, transcendentals=0),
        name="forward",
    )(current, radiate, interp, cosine, sine, lists)


def translate_kernel(lay, n_kind, got_ref, table_ref, out_ref, x_ref, t_ref, acc_ref):
    n_par = got_ref.shape[0]
    span = 2 * lay.pad
    n_pad = table_ref.shape[1]
    got = got_ref[...].T
    high, low = halves(got[0:span])
    x_ref[0:span] = high
    x_ref[span:2 * span] = low
    high, low = halves(table_ref[...])
    t_ref[0:span] = high
    t_ref[span:2 * span] = low
    codes = got[lay.lists:lay.lists + lay.list_len].astype(jnp.int32)
    width = min(512, n_par)
    rows_src = iota((n_par, width), 0)
    rows_kind = iota((n_pad, width), 0)
    for p in range(0, n_par, width):
        re_sum = im_sum = None
        for m in range(lay.list_len):
            code = codes[m:m + 1, p:p + width]
            source = jnp.right_shift(code, 9)
            kind = jnp.bitwise_and(code, 511)
            pick = (rows_src == source).astype(BF16)
            both = dot_nn(x_ref[...], pick)
            chosen = both[0:span] + both[span:2 * span]
            pick = (rows_kind == kind).astype(BF16)
            both = dot_nn(t_ref[...], pick)
            factor = both[0:span] + both[span:2 * span]
            fr, fi = factor[0:lay.pad], factor[lay.pad:span]
            cr, ci = chosen[0:lay.pad], chosen[lay.pad:span]
            re = fr * cr - fi * ci
            im = fr * ci + fi * cr
            re_sum = re if m == 0 else re_sum + re
            im_sum = im if m == 0 else im_sum + im
        acc_ref[0:lay.pad, p:p + width] = re_sum
        acc_ref[lay.pad:span, p:p + width] = im_sum
    acc_ref[span:128] = jnp.zeros((128 - span, n_par), F32)
    out_ref[...] = acc_ref[...].T


def translate_far(lay, got, table, n_kind):
    n_par = got.shape[0]
    span = 2 * lay.pad
    return pl.pallas_call(
        functools.partial(translate_kernel, lay, n_kind),
        out_shape=jax.ShapeDtypeStruct((n_par, 128), F32),
        scratch_shapes=[
            pltpu.VMEM((2 * span, n_par), BF16),
            pltpu.VMEM((2 * span, table.shape[1]), BF16),
            pltpu.VMEM((128, n_par), F32),
        ],
        compiler_params=pltpu.CompilerParams(vmem_limit_bytes=VMEM_LIMIT),
        cost_estimate=pl.CostEstimate(flops=4 * 10**9, bytes_accessed=10**6, transcendentals=0),
        name="translate_far",
    )(got, table)


def backward_kernel(lay, got_ref, interp_ref, rec_ref, cos_ref, sin_ref, near_ref, out_ref,
                    inc_ref, high_ref, low_ref):
    step = pl.program_id(0)
    n_par = got_ref.shape[1]
    count = 8 * n_par

    @pl.when(step == 0)
    def _():
        for dest in range(lay.n_dev):
            j = lay.first(dest)
            inc_ref[0, :, j:j + lay.own] = got_ref[dest, :, 0:lay.own]
            inc_ref[1, :, j:j + lay.own] = got_ref[dest, :, lay.pad:lay.pad + lay.own]
        c = cos_ref[...]
        s = sin_ref[...]
        for p in range(0, n_par, 2):
            res, ims = [], []
            for q in (p, p + 1):
                re = inc_ref[0, q:q + 1, :]
                im = inc_ref[1, q:q + 1, :]
                res.append(c * re + s * im)
                ims.append(c * im - s * re)
            high, low = halves(jnp.concatenate(res, axis=0))
            high_ref[8 * p:8 * p + 16] = high
            low_ref[8 * p:8 * p + 16] = low
            high, low = halves(jnp.concatenate(ims, axis=0))
            high_ref[count + 8 * p:count + 8 * p + 16] = high
            low_ref[count + 8 * p:count + 8 * p + 16] = low
        out_ref[...] = near_ref[...]

    in_high, in_low = halves(interp_ref[...])
    leaf = dot_nn(high_ref[...], in_high) + dot_nn(high_ref[...], in_low) + dot_nn(low_ref[...], in_high)
    leaf_high, leaf_low = halves(leaf)
    rr_high, rr_low = halves(rec_ref[0])
    ri_high, ri_low = halves(rec_ref[1])
    by_re = dot_nn(leaf_high, rr_high) + dot_nn(leaf_high, rr_low) + dot_nn(leaf_low, rr_high)
    by_im = dot_nn(leaf_high, ri_high) + dot_nn(leaf_high, ri_low) + dot_nn(leaf_low, ri_high)
    out_ref[0] += by_re[0:count] - by_im[count:2 * count]
    out_ref[1] += by_im[0:count] + by_re[count:2 * count]


def backward(lay, got, interp, receive, cosine, sine, near):
    n_par = got.shape[1]
    count = 8 * n_par
    k_up, k_leaf = interp.shape
    unk = receive.shape[2]
    width = 256
    whole = lambda *shape: pl.BlockSpec(shape, lambda i: (0,) * len(shape))
    return pl.pallas_call(
        functools.partial(backward_kernel, lay),
        grid=(k_leaf // width,),
        in_specs=[
            whole(lay.n_dev, n_par, 128),
            pl.BlockSpec((k_up, width), lambda i: (0, i)),
            pl.BlockSpec((2, width, unk), lambda i: (0, i, 0)),
            whole(8, k_up),
            whole(8, k_up),
            whole(2, count, unk),
        ],
        out_specs=whole(2, count, unk),
        out_shape=jax.ShapeDtypeStruct((2, count, unk), F32),
        scratch_shapes=[
            pltpu.VMEM((2, n_par, k_up), F32),
            pltpu.VMEM((2 * count, k_up), BF16),
            pltpu.VMEM((2 * count, k_up), BF16),
        ],
        compiler_params=pltpu.CompilerParams(vmem_limit_bytes=VMEM_LIMIT),
        cost_estimate=pl.CostEstimate(flops=3 * 10**9, bytes_accessed=9 * 10**6, transcendentals=0),
        name="backward",
    )(got, interp, receive, cosine, sine, near)


def near_kernel(n_block, cols_ref, rows_ref, cur_ref, blocks_ref, out_ref, pick_ref, own_ref):
    step = pl.program_id(0)
    here = blocks_ref.shape[0]
    unk = blocks_ref.shape[2]
    slots, _, group, _ = cur_ref.shape

    @pl.when(step == 0)
    def _():
        col = cols_ref[...]
        for part in range(2):
            total = jnp.zeros((64, unk), F32)
            for slot in range(slots):
                mark = (iota((64, group), 1) + slot * group == col).astype(BF16)
                total = total + dot_nn(mark, cur_ref[slot, part])
            pick_ref[64 * part:64 * part + 64] = total.astype(BF16)
        own_ref[...] = jnp.zeros_like(own_ref)

    lane = iota((2 * unk, 128), 1) % 64
    own = own_ref[...]
    for i in range(here):
        block = blocks_ref[i].reshape(2 * unk, unk)
        own = jnp.where(lane == step * here + i, dot_nt(block, pick_ref[...]), own)
    own_ref[...] = own

    @pl.when(step == pl.num_programs(0) - 1)
    def _():
        by_block = own_ref[...].T
        by_re, by_im = by_block[:, 0:unk], by_block[:, unk:2 * unk]
        re = by_re[0:64] - by_im[64:128]
        im = by_re[64:128] + by_im[0:64]
        count = out_ref.shape[1]
        mark = (iota((count, 64), 0) == rows_ref[...]).astype(BF16)
        for part, value in ((0, re), (1, im)):
            high, low = halves(value)
            out_ref[part] = dot_nn(mark, high) + dot_nn(mark, low)


def near_field(cols, rows, gathered, blocks, count):
    n_block, _, unk, _ = blocks.shape
    here = 8
    whole = lambda *shape: pl.BlockSpec(shape, lambda i: (0,) * len(shape))
    return pl.pallas_call(
        functools.partial(near_kernel, n_block),
        grid=(n_block // here,),
        in_specs=[
            whole(64, 1),
            whole(1, 64),
            whole(*gathered.shape),
            pl.BlockSpec((here, 2, unk, unk), lambda i: (i, 0, 0, 0)),
        ],
        out_specs=whole(2, count, unk),
        out_shape=jax.ShapeDtypeStruct((2, count, unk), F32),
        scratch_shapes=[
            pltpu.VMEM((128, unk), BF16),
            pltpu.VMEM((2 * unk, 128), F32),
        ],
        compiler_params=pltpu.CompilerParams(vmem_limit_bytes=VMEM_LIMIT),
        cost_estimate=pl.CostEstimate(flops=2 * 10**9, bytes_accessed=12 * 10**6, transcendentals=0),
        name="near_field",
    )(cols, rows, gathered, blocks)


def on_device(n_grp, n_ang, current, near_blocks, near_rows, near_cols, radiate, receive, interp,
              shift_phase, translate, far_sources, far_types):
    count, unk = current.shape[1:]
    n_par = count // 8
    n_block = near_blocks.shape[0]
    k_up = interp.shape[0]
    n_kind = translate.shape[1]
    lay = Layout(n_grp, n_ang, k_up, far_sources.shape[1])
    grp = lax.axis_index("grp")
    ang = lax.axis_index("ang")
    axes = ("grp", "ang")

    swapped = lax.ppermute(current, "ang", [(i, i ^ 1) for i in range(n_ang)])
    pair = jnp.concatenate([current, swapped], axis=1)
    sides = [[i for i in range(n_ang) if i % 2 == side] for side in range(2)]
    gathered = lax.all_gather(pair, "ang", axis_index_groups=sides)

    cosine = jnp.cos(shift_phase)
    sine = jnp.sin(shift_phase)
    own_src = lax.dynamic_slice_in_dim(far_sources, ang * n_par, n_par, 0)
    own_kind = lax.dynamic_slice_in_dim(far_types, ang * n_par, n_par, 0)
    lists = (own_src * 512 + own_kind).astype(F32)

    message = forward(lay, current, radiate, interp, cosine, sine, lists)
    got = lax.all_to_all(message, axes, 0, 0)

    table = lax.dynamic_slice_in_dim(translate, grp * lay.own, lay.own, 2)
    kind_pad = -(-n_kind // 128) * 128
    table = jnp.pad(table, ((0, 0), (0, kind_pad - n_kind), (0, lay.pad - lay.own)))
    table = jnp.transpose(table, (0, 2, 1)).reshape(2 * lay.pad, kind_pad)

    incoming = translate_far(lay, got.reshape(lay.n_dev * n_par, 128), table, n_kind)
    returned = lax.all_to_all(incoming.reshape(lay.n_dev, n_par, 128), axes, 0, 0)

    owner = near_cols // count
    place = (owner // 2) * 2 * count + ((owner % 2) ^ (ang % 2)) * count + near_cols % count
    cols = jnp.full((64, 1), -1, jnp.int32).at[:n_block, 0].set(place)
    rows = jnp.full((1, 64), -1, jnp.int32).at[0, :n_block].set(near_rows)
    near = near_field(cols, rows, gathered, near_blocks, count)

    return backward(lay, returned, interp, receive, cosine, sine, near)


def solution(mesh):
    both = ("grp", "ang")
    in_specs = (
        P(None, both, None),
        P(both, None, None, None),
        P(both),
        P(both),
        P(),
        P(),
        P(),
        P(),
        P(None, None, "ang"),
        P("grp", None),
        P("grp", None),
    )
    run = functools.partial(on_device, mesh.shape["grp"], mesh.shape["ang"])
    return jax.shard_map(run, mesh=mesh, in_specs=in_specs, out_specs=P(None, both, None), check_vma=False)
```

```python
import functools
import jax
import jax.numpy as jnp
from jax import lax
from jax.experimental import pallas as pl
from jax.experimental.pallas import tpu as pltpu
from jax.sharding import PartitionSpec as P

F32 = jnp.float32
BF16 = jnp.bfloat16
VMEM_LIMIT = 24 << 20
HBM = pl.BlockSpec(memory_space=pltpu.HBM)
VMEM = pl.BlockSpec(memory_space=pltpu.VMEM)
SMEM = pl.BlockSpec(memory_space=pltpu.SMEM)
TILE = 512


def halves(x):
    high = x.astype(BF16)
    return high, (x - high.astype(F32)).astype(BF16)


def dot_nt(a, b):
    return lax.dot_general(a, b, (((1,), (1,)), ((), ())), preferred_element_type=F32)


def dot_nn(a, b):
    return lax.dot_general(a, b, (((1,), (0,)), ((), ())), preferred_element_type=F32)


def in_hbm(x):
    return pltpu.with_memory_space_constraint(x, pltpu.HBM)


def iota(shape, dim):
    return lax.broadcasted_iota(jnp.int32, shape, dim)


class Layout:
    def __init__(self, n_grp, n_ang, k_up, list_len):
        self.n_grp, self.n_ang = n_grp, n_ang
        self.n_dev = n_grp * n_ang
        self.own = k_up // self.n_dev
        self.pad = -(-self.own // 8) * 8
        self.list_len = list_len

    def first(self, dest):
        grp, ang = divmod(dest, self.n_ang)
        return (ang * self.n_grp + grp) * self.own


HALF = 64
NOTES = 48
CODE_BITS = 20
BIAS = 2048


def exponent(largest):
    return jnp.ceil(8.0 * jnp.log2(jnp.maximum(largest, 1e-30)))


def scale_of(eighths):
    return jnp.exp2(eighths * 0.125)


def pack(re, im, scale):
    def grid(x):
        return jnp.clip(jnp.round(x * (32767.0 / scale)), -32767.0, 32767.0).astype(jnp.int32)
    return jnp.bitwise_or(jnp.left_shift(grid(re), 16), jnp.bitwise_and(grid(im), 65535))


def unpack(words, scale):
    step = scale * (1.0 / 32767.0)
    re = jnp.right_shift(words, 16).astype(F32) * step
    im = jnp.right_shift(jnp.left_shift(words, 16), 16).astype(F32) * step
    return re, im


def note(word):
    return lax.shift_right_logical(word, CODE_BITS)


def fetch(source, target, sems, dim):
    def piece(i):
        at = (slice(None),) * dim + (pl.ds(pl.multiple_of(i * TILE, TILE), TILE),)
        return pltpu.make_async_copy(source.at[at], target.at[at], sems.at[i])

    for i in range(source.shape[dim] // TILE):
        piece(i).start()
    return lambda i: piece(i).wait()


def forward_kernel(lay, ang_ref, cur_hbm, phase_hbm, src_hbm, kind_hbm, cols_hbm, rad_hbm, interp_hbm, out_ref, cos_ref,
                   sin_ref, cur_ref, phase_ref, src_ref, kind_ref, cols_ref, rad_ref, interp_ref, high_ref, low_ref,
                   par_ref, code_ref, small_sems, rad_sems, interp_sems):
    small = [
        pltpu.make_async_copy(source, target, small_sems.at[i])
        for i, (source, target) in enumerate([
            (cur_hbm, cur_ref), (phase_hbm, phase_ref), (src_hbm, src_ref), (kind_hbm, kind_ref),
            (cols_hbm, cols_ref)])
    ]
    for copy in small:
        copy.start()
    rad_wait = fetch(rad_hbm, rad_ref, rad_sems, 1)
    interp_wait = fetch(interp_hbm, interp_ref, interp_sems, 0)
    for copy in small:
        copy.wait()
    count = cur_ref.shape[1]
    n_par = count // 8
    k_up, k_leaf = interp_ref.shape

    row = iota((count, count), 0)
    col = iota((count, count), 1)
    order = (col == (row % n_par) * 8 + row // n_par).astype(BF16)
    cur_re = dot_nn(order, cur_ref[0]).astype(BF16)
    cur_im = dot_nn(order, cur_ref[1]).astype(BF16)
    left = jnp.concatenate([cur_re, cur_im], axis=0)
    right = jnp.concatenate([-cur_im, cur_re], axis=0)
    cos_ref[...] = jnp.cos(phase_ref[...])
    sin_ref[...] = jnp.sin(phase_ref[...])

    src = src_ref[...]
    place = (jnp.left_shift(jnp.right_shift(src, 4), 3) + jnp.bitwise_and(src, 7)
             + jnp.bitwise_and(jnp.right_shift(src, 3), 1) * (lay.n_dev * n_par // 2))
    code_ref[:, 0:lay.list_len] = (place * 512 + kind_ref[...]).T
    codes = code_ref[pl.ds(pl.multiple_of(ang_ref[0] * n_par, n_par), n_par), 0:lay.list_len]
    n_ask = cols_ref.shape[1]
    asks = jnp.concatenate([cols_ref[...], jnp.zeros((1, 128 - n_ask), jnp.int32)], axis=1)
    asks = jnp.broadcast_to(asks, (8, 128)).T[:, 0:1]
    asks = [asks[b:b + n_par] for b in range(0, n_ask, n_par)]

    for i in range(k_leaf // TILE):
        rad_wait(i)
        at = pl.ds(i * TILE, TILE)
        rr_high, rr_low = halves(rad_ref[0, at, :])
        ri_high, ri_low = halves(rad_ref[1, at, :])
        radiated = (dot_nt(left, rr_high) + dot_nt(left, rr_low)
                    + dot_nt(right, ri_high) + dot_nt(right, ri_low))
        high, low = halves(radiated)
        high_ref[:, at] = high
        low_ref[:, at] = low

    for i in range(k_up // TILE):
        interp_wait(i)
        at = pl.ds(i * TILE, TILE)
        in_high, in_low = halves(interp_ref[at, :])
        children = (dot_nt(high_ref[...], in_high) + dot_nt(high_ref[...], in_low)
                    + dot_nt(low_ref[...], in_high))
        re_sum = im_sum = None
        for t in range(8):
            c = cos_ref[t:t + 1, at]
            s = sin_ref[t:t + 1, at]
            re = children[t * n_par:(t + 1) * n_par]
            im = children[count + t * n_par:count + (t + 1) * n_par]
            re_t = c * re - s * im
            im_t = c * im + s * re
            re_sum = re_t if t == 0 else re_sum + re_t
            im_sum = im_t if t == 0 else im_sum + im_t
        par_ref[0, :, at] = re_sum
        par_ref[1, :, at] = im_sum

    largest = jnp.max(jnp.maximum(jnp.abs(par_ref[0]), jnp.abs(par_ref[1])), axis=1, keepdims=True)
    eighths = exponent(largest)
    words = pack(par_ref[0], par_ref[1], scale_of(eighths))
    notes = [eighths.astype(jnp.int32) + BIAS] + asks
    notes.append(jnp.zeros((n_par, lay.list_len - len(notes)), jnp.int32))
    notes = codes + jnp.left_shift(jnp.concatenate(notes, axis=1), CODE_BITS)
    gap = [jnp.zeros((8, NOTES - lay.own), jnp.int32)] if lay.own < NOTES else []
    for dest in range(lay.n_dev):
        at = slice(lay.first(dest), lay.first(dest) + lay.own)
        out_ref[dest] = jnp.concatenate(
            [words[0:8, at], *gap, notes[0:8], words[8:16, at], *gap, notes[8:16]], axis=1)


def forward(lay, ang, current, radiate, interp, phase, sources, types, cols):
    count = current.shape[1]
    k_up, k_leaf = interp.shape
    n_par = count // 8
    return pl.pallas_call(
        functools.partial(forward_kernel, lay),
        in_specs=[SMEM] + [HBM] * 7,
        out_specs=[VMEM] * 3,
        out_shape=[
            jax.ShapeDtypeStruct((lay.n_dev, 8, 128), jnp.int32),
            jax.ShapeDtypeStruct(phase.shape, F32),
            jax.ShapeDtypeStruct(phase.shape, F32),
        ],
        scratch_shapes=[
            pltpu.VMEM(current.shape, BF16),
            pltpu.VMEM(phase.shape, F32),
            pltpu.VMEM(sources.shape[::-1], jnp.int32),
            pltpu.VMEM(types.shape[::-1], jnp.int32),
            pltpu.VMEM(cols.shape, jnp.int32),
            pltpu.VMEM(radiate.shape, F32),
            pltpu.VMEM(interp.shape, F32),
            pltpu.VMEM((2 * count, k_leaf), BF16),
            pltpu.VMEM((2 * count, k_leaf), BF16),
            pltpu.VMEM((2, n_par, k_up), F32),
            pltpu.VMEM((sources.shape[0], 128), jnp.int32),
            pltpu.SemaphoreType.DMA((5,)),
            pltpu.SemaphoreType.DMA((k_leaf // TILE,)),
            pltpu.SemaphoreType.DMA((k_up // TILE,)),
        ],
        compiler_params=pltpu.CompilerParams(vmem_limit_bytes=VMEM_LIMIT),
        cost_estimate=pl.CostEstimate(flops=3 * 10**9, bytes_accessed=9 * 10**6, transcendentals=0),
        name="forward",
    )(ang, *map(in_hbm, (current, phase, sources.T, types.T, cols, radiate, interp)))


def translate_kernel(lay, got_ref, table_ref, out_ref, x_ref, t_ref, acc_ref):
    n_par = 2 * got_ref.shape[0]
    side = n_par // 2
    span = 2 * lay.pad
    n_pad = table_ref.shape[1]
    got = got_ref[...].T
    codes = []
    for h in range(2):
        words = got[HALF * h:HALF * h + lay.pad]
        codes.append(got[HALF * h + NOTES:HALF * h + NOTES + lay.list_len])
        scale = scale_of((note(codes[h][0:1]) - BIAS).astype(F32))
        for part, value in enumerate(unpack(words, scale)):
            high, low = halves(value)
            at = lay.pad * part
            x_ref[at:at + lay.pad, side * h:side * h + side] = high
            x_ref[span + at:span + at + lay.pad, side * h:side * h + side] = low
    codes = jnp.bitwise_and(jnp.concatenate(codes, axis=1), (1 << CODE_BITS) - 1)
    high, low = halves(table_ref[...])
    t_ref[0:span] = high
    t_ref[span:2 * span] = low
    width = min(512, n_par)
    rows_src = iota((n_par, width), 0)
    rows_kind = iota((n_pad, width), 0)
    for p in range(0, n_par, width):
        at = slice(p, p + width)
        re_sum = im_sum = 0.0
        for m in range(lay.list_len):
            code = codes[m:m + 1, at]
            source = jnp.right_shift(code, 9)
            kind = jnp.bitwise_and(code, 511)
            pick = (rows_src == source).astype(BF16)
            both = dot_nn(x_ref[...], pick)
            chosen = both[0:span] + both[span:2 * span]
            pick = (rows_kind == kind).astype(BF16)
            both = dot_nn(t_ref[...], pick)
            factor = both[0:span] + both[span:2 * span]
            fr, fi = factor[0:lay.pad], factor[lay.pad:span]
            cr, ci = chosen[0:lay.pad], chosen[lay.pad:span]
            re_sum = re_sum + (fr * cr - fi * ci)
            im_sum = im_sum + (fr * ci + fi * cr)
        largest = jnp.maximum(jnp.max(jnp.abs(re_sum), axis=0, keepdims=True),
                              jnp.max(jnp.abs(im_sum), axis=0, keepdims=True))
        eighths = exponent(largest)
        acc_ref[0:lay.pad, at] = pack(re_sum, im_sum, scale_of(eighths))
        acc_ref[NOTES:NOTES + 8, at] = jnp.broadcast_to(eighths, (8, width)).astype(jnp.int32)
    for h in range(2):
        out_ref[:, HALF * h:HALF * h + HALF] = acc_ref[:, side * h:side * h + side].T


def translate_far(lay, got, table):
    n_par = 2 * got.shape[0]
    span = 2 * lay.pad
    return pl.pallas_call(
        functools.partial(translate_kernel, lay),
        in_specs=[VMEM] * 2,
        out_specs=VMEM,
        out_shape=jax.ShapeDtypeStruct(got.shape, jnp.int32),
        scratch_shapes=[
            pltpu.VMEM((2 * span, n_par), BF16),
            pltpu.VMEM((2 * span, table.shape[1]), BF16),
            pltpu.VMEM((HALF, n_par), jnp.int32),
        ],
        compiler_params=pltpu.CompilerParams(vmem_limit_bytes=VMEM_LIMIT),
        cost_estimate=pl.CostEstimate(flops=2 * 10**9, bytes_accessed=10**6, transcendentals=0),
        name="translate_far",
    )(got, table)


def backward_kernel(lay, got_ref, cos_ref, sin_ref, near_ref, interp_hbm, rec_hbm, out_ref,
                    interp_ref, rec_ref, inc_ref, high_ref, low_ref, interp_sems, rec_sems):
    interp_wait = fetch(interp_hbm, interp_ref, interp_sems, 1)
    rec_wait = fetch(rec_hbm, rec_ref, rec_sems, 1)
    count = near_ref.shape[1]
    n_par = count // 8

    for dest in range(lay.n_dev):
        words = got_ref[dest]
        j = lay.first(dest)
        for h in range(2):
            eighths = words[:, HALF * h + NOTES:HALF * h + NOTES + 1].astype(F32)
            values = unpack(words[:, HALF * h:HALF * h + lay.own], scale_of(eighths))
            for part in range(2):
                inc_ref[part, 8 * h:8 * h + 8, j:j + lay.own] = values[part]
    c = cos_ref[...]
    s = sin_ref[...]
    for p in range(0, n_par, 2):
        res, ims = [], []
        for q in (p, p + 1):
            re = inc_ref[0, q:q + 1, :]
            im = inc_ref[1, q:q + 1, :]
            res.append(c * re + s * im)
            ims.append(c * im - s * re)
        high, low = halves(jnp.concatenate(res, axis=0))
        high_ref[8 * p:8 * p + 16] = high
        low_ref[8 * p:8 * p + 16] = low
        high, low = halves(jnp.concatenate(ims, axis=0))
        high_ref[count + 8 * p:count + 8 * p + 16] = high
        low_ref[count + 8 * p:count + 8 * p + 16] = low

    re_sum, im_sum = near_ref[0], near_ref[1]
    for i in range(interp_ref.shape[1] // TILE):
        interp_wait(i)
        at = slice(i * TILE, i * TILE + TILE)
        in_high, in_low = halves(interp_ref[:, at])
        leaf = dot_nn(high_ref[...], in_high) + dot_nn(high_ref[...], in_low) + dot_nn(low_ref[...], in_high)
        leaf_high, leaf_low = halves(leaf)
        rec_wait(i)
        by = []
        for part in range(2):
            rec_high, rec_low = halves(rec_ref[part, at, :])
            by.append(dot_nn(leaf_high, rec_high) + dot_nn(leaf_high, rec_low) + dot_nn(leaf_low, rec_high))
        re_sum = re_sum + (by[0][0:count] - by[1][count:2 * count])
        im_sum = im_sum + (by[1][0:count] + by[0][count:2 * count])
    out_ref[0] = re_sum
    out_ref[1] = im_sum


def backward(lay, got, interp, receive, cosine, sine, near):
    count = near.shape[1]
    n_par = count // 8
    k_up, k_leaf = interp.shape
    unk = receive.shape[2]
    return pl.pallas_call(
        functools.partial(backward_kernel, lay),
        in_specs=[VMEM] * 4 + [HBM] * 2,
        out_specs=VMEM,
        out_shape=jax.ShapeDtypeStruct((2, count, unk), F32),
        scratch_shapes=[
            pltpu.VMEM(interp.shape, F32),
            pltpu.VMEM(receive.shape, F32),
            pltpu.VMEM((2, n_par, k_up), F32),
            pltpu.VMEM((2 * count, k_up), BF16),
            pltpu.VMEM((2 * count, k_up), BF16),
            pltpu.SemaphoreType.DMA((k_leaf // TILE,)),
            pltpu.SemaphoreType.DMA((k_leaf // TILE,)),
        ],
        compiler_params=pltpu.CompilerParams(vmem_limit_bytes=VMEM_LIMIT),
        cost_estimate=pl.CostEstimate(flops=3 * 10**9, bytes_accessed=9 * 10**6, transcendentals=0),
        name="backward",
    )(got, cosine, sine, near, in_hbm(interp), in_hbm(receive))


def pick_kernel(lay, n_block, me_ref, got_ref, cur_ref, *out_refs):
    count = cur_ref.shape[1]
    first = me_ref[0]
    ang = me_ref[1]
    for mask, out_ref in enumerate(out_refs):
        dest = first + jnp.bitwise_xor(ang, mask)
        notes = note(got_ref[dest])
        marks = []
        for field in range(1, 1 + -(-n_block // 16)):
            for h in range(2):
                lane = HALF * h + NOTES + field
                marks.append((iota((8, count), 1) == notes[:, lane:lane + 1] - ang * count).astype(F32))
        mark = jnp.concatenate(marks, axis=0).astype(BF16)
        for part in range(2):
            out_ref[part] = dot_nn(mark, cur_ref[part]).astype(BF16)


def pick_columns(lay, n_block, me, got, current):
    unk = current.shape[2]
    rows = -(-n_block // 16) * 16
    one = jax.ShapeDtypeStruct((2, rows, unk), BF16)
    return pl.pallas_call(
        functools.partial(pick_kernel, lay, n_block),
        in_specs=[SMEM, VMEM, VMEM],
        out_specs=[VMEM] * lay.n_ang,
        out_shape=[one] * lay.n_ang,
        compiler_params=pltpu.CompilerParams(vmem_limit_bytes=VMEM_LIMIT),
        cost_estimate=pl.CostEstimate(flops=10**8, bytes_accessed=10**6, transcendentals=0),
        name="pick_columns",
    )(me, got, current)


def swap(picked, n_ang):
    half = [picked[mask] for mask in range(0, n_ang, 2)]
    sent = jnp.stack([picked[mask] for mask in range(1, n_ang, 2)])
    got = lax.ppermute(sent, "ang", [(i, i ^ 1) for i in range(n_ang)])
    return [one + got[k] for k, one in enumerate(half)]


def answers(half, n_ang):
    return [half[0]] + [
        lax.ppermute(half[k], "ang", [(i, i ^ (2 * k)) for i in range(n_ang)]) for k in range(1, len(half))
    ]


def near_kernel(n_term, *refs):
    rows_ref, terms, (blocks_hbm, out_ref, blocks_ref, wide_ref, own_ref, sems) = (
        refs[0], refs[1:1 + n_term], refs[1 + n_term:])
    n_block, _, unk, _ = blocks_ref.shape
    here = n_block // sems.shape[0]

    def piece(i):
        at = pl.ds(i * here, here)
        return pltpu.make_async_copy(blocks_hbm.at[at], blocks_ref.at[at], sems.at[i])

    for i in range(sems.shape[0]):
        piece(i).start()
    wide_ref[...] = jnp.zeros_like(wide_ref)
    for part in range(2):
        total = terms[0][part].astype(F32)
        for term in terms[1:]:
            total = total + term[part].astype(F32)
        wide_ref[64 * part:64 * part + total.shape[0]] = total.astype(BF16)
    lane = iota((2 * unk, 128), 1) % 64
    own = jnp.zeros((2 * unk, 128), F32)
    for i in range(0, n_block, here):
        piece(i // here).wait()
        rows = blocks_ref[i:i + here].reshape(here * 2 * unk, unk)
        products = dot_nt(rows, wide_ref[...])
        for k in range(here):
            own = jnp.where(lane == i + k, products[2 * unk * k:2 * unk * (k + 1)], own)
    own_ref[...] = own

    by_block = own_ref[...].T
    by_re, by_im = by_block[:, 0:unk], by_block[:, unk:2 * unk]
    re = by_re[0:n_block] - by_im[64:64 + n_block]
    im = by_re[64:64 + n_block] + by_im[0:n_block]
    count = out_ref.shape[1]
    mark = (iota((count, n_block), 0) == rows_ref[...]).astype(BF16)
    for part, value in ((0, re), (1, im)):
        high, low = halves(value)
        out_ref[part] = dot_nn(mark, high) + dot_nn(mark, low)


def near_field(rows, terms, blocks, count):
    n_block, _, unk, _ = blocks.shape
    here = 4
    return pl.pallas_call(
        functools.partial(near_kernel, len(terms)),
        in_specs=[VMEM] * (1 + len(terms)) + [HBM],
        out_specs=VMEM,
        out_shape=jax.ShapeDtypeStruct((2, count, unk), F32),
        scratch_shapes=[
            pltpu.VMEM(blocks.shape, BF16),
            pltpu.VMEM((128, unk), BF16),
            pltpu.VMEM((2 * unk, 128), F32),
            pltpu.SemaphoreType.DMA((n_block // here,)),
        ],
        compiler_params=pltpu.CompilerParams(vmem_limit_bytes=VMEM_LIMIT),
        cost_estimate=pl.CostEstimate(flops=2 * 10**11, bytes_accessed=12 * 10**6, transcendentals=0),
        name="near_field",
    )(rows, *terms, in_hbm(blocks))


def on_device(n_grp, n_ang, current, near_blocks, near_rows, near_cols, radiate, receive, interp,
              shift_phase, translate, far_sources, far_types):
    count, unk = current.shape[1:]
    n_par = count // 8
    n_block = near_blocks.shape[0]
    k_up = interp.shape[0]
    n_kind = translate.shape[1]
    lay = Layout(n_grp, n_ang, k_up, far_sources.shape[1])
    grp = lax.axis_index("grp")
    ang = lax.axis_index("ang")
    axes = ("grp", "ang")

    message, cosine, sine = forward(
        lay, ang[None], current, radiate, interp, shift_phase, far_sources, far_types, near_cols[None])
    got = lax.all_to_all(message, axes, 0, 0)
    half = swap(pick_columns(lay, n_block, jnp.stack([grp * n_ang, ang]), got, current), n_ang)

    table = lax.dynamic_slice_in_dim(translate, grp * lay.own, lay.own, 2)
    kind_pad = -(-n_kind // 128) * 128
    table = jnp.pad(table, ((0, 0), (0, kind_pad - n_kind), (0, lay.pad - lay.own)))
    table = jnp.transpose(table, (0, 2, 1)).reshape(2 * lay.pad, kind_pad)

    incoming = translate_far(lay, got.reshape(lay.n_dev * 8, 128), table)
    incoming, half = lax.optimization_barrier((incoming, half))
    near = near_field(near_rows[None], answers(half, n_ang), near_blocks, count)
    returned = lax.all_to_all(incoming.reshape(lay.n_dev, 8, 128), axes, 0, 0)

    return backward(lay, returned, interp, receive, cosine, sine, near)


def solution(mesh):
    both = ("grp", "ang")
    in_specs = (
        P(None, both, None),
        P(both, None, None, None),
        P(both),
        P(both),
        P(),
        P(),
        P(),
        P(),
        P(None, None, "ang"),
        P("grp", None),
        P("grp", None),
    )
    run = functools.partial(on_device, mesh.shape["grp"], mesh.shape["ang"])
    return jax.shard_map(run, mesh=mesh, in_specs=in_specs, out_specs=P(None, both, None), check_vma=False)
```

```python
import functools
import jax
import jax.numpy as jnp
from jax import lax
from jax.experimental import pallas as pl
from jax.experimental.pallas import tpu as pltpu
from jax.sharding import PartitionSpec as P

F32 = jnp.float32
BF16 = jnp.bfloat16
VMEM_LIMIT = 24 << 20
HBM = pl.BlockSpec(memory_space=pltpu.HBM)
VMEM = pl.BlockSpec(memory_space=pltpu.VMEM)
SMEM = pl.BlockSpec(memory_space=pltpu.SMEM)
TILE = 512
ROWS = 512


def halves(x):
    high = x.astype(BF16)
    return high, (x - high.astype(F32)).astype(BF16)


def dot_nt(a, b):
    return lax.dot_general(a, b, (((1,), (1,)), ((), ())), preferred_element_type=F32)


def dot_nn(a, b):
    return lax.dot_general(a, b, (((1,), (0,)), ((), ())), preferred_element_type=F32)


def in_hbm(x):
    return pltpu.with_memory_space_constraint(x, pltpu.HBM)


def iota(shape, dim):
    return lax.broadcasted_iota(jnp.int32, shape, dim)


class Layout:
    def __init__(self, n_grp, n_ang, k_up, list_len):
        self.n_grp, self.n_ang = n_grp, n_ang
        self.n_dev = n_grp * n_ang
        self.own = k_up // self.n_dev
        self.pad = -(-self.own // 8) * 8
        self.list_len = list_len

    def first(self, dest):
        grp, ang = divmod(dest, self.n_ang)
        return (ang * self.n_grp + grp) * self.own


HALF = 64
NOTES = 48
CODE_BITS = 20
BIAS = 2048


def exponent(largest):
    return jnp.ceil(8.0 * jnp.log2(jnp.maximum(largest, 1e-30)))


def scale_of(eighths):
    return jnp.exp2(eighths * 0.125)


def pack(re, im, scale):
    def grid(x):
        return jnp.clip(jnp.round(x * (32767.0 / scale)), -32767.0, 32767.0).astype(jnp.int32)
    return jnp.bitwise_or(jnp.left_shift(grid(re), 16), jnp.bitwise_and(grid(im), 65535))


def unpack(words, scale):
    step = scale * (1.0 / 32767.0)
    re = jnp.right_shift(words, 16).astype(F32) * step
    im = jnp.right_shift(jnp.left_shift(words, 16), 16).astype(F32) * step
    return re, im


def note(word):
    return lax.shift_right_logical(word, CODE_BITS)


def piece(source, target, sems, dim, size):
    def at(i):
        index = (slice(None),) * dim + (pl.ds(pl.multiple_of(i * size, size), size),)
        return pltpu.make_async_copy(source.at[index], target.at[index], sems.at[i])
    return at


def forward_kernel(lay, ang_ref, cur_hbm, phase_hbm, src_hbm, kind_hbm, cols_hbm, rad_hbm, interp_hbm, out_ref, cos_ref,
                   sin_ref, cur_ref, phase_ref, src_ref, kind_ref, cols_ref, rad_ref, interp_ref, high_ref, low_ref,
                   par_ref, code_ref, small_sems, rad_sems, interp_sems):
    small = [
        pltpu.make_async_copy(source, target, small_sems.at[i])
        for i, (source, target) in enumerate([
            (cur_hbm, cur_ref), (phase_hbm, phase_ref), (src_hbm, src_ref), (kind_hbm, kind_ref),
            (cols_hbm, cols_ref)])
    ]
    for copy in small:
        copy.start()
    rad_piece = piece(rad_hbm, rad_ref, rad_sems, 1, TILE)
    interp_piece = piece(interp_hbm, interp_ref, interp_sems, 0, ROWS)
    n_rad, n_interp = rad_sems.shape[0], interp_sems.shape[0]
    for i in range(n_rad):
        rad_piece(i).start()
    interp_piece(0).start()
    for copy in small:
        copy.wait()
    count = cur_ref.shape[1]
    n_par = count // 8
    k_up, k_leaf = interp_ref.shape

    row = iota((count, count), 0)
    col = iota((count, count), 1)
    order = (col == (row % n_par) * 8 + row // n_par).astype(BF16)
    cur_re = dot_nn(order, cur_ref[0]).astype(BF16)
    cur_im = dot_nn(order, cur_ref[1]).astype(BF16)
    left = jnp.concatenate([cur_re, cur_im], axis=0)
    right = jnp.concatenate([-cur_im, cur_re], axis=0)
    cos_ref[...] = jnp.cos(phase_ref[...])
    sin_ref[...] = jnp.sin(phase_ref[...])

    src = src_ref[...]
    place = (jnp.left_shift(jnp.right_shift(src, 4), 3) + jnp.bitwise_and(src, 7)
             + jnp.bitwise_and(jnp.right_shift(src, 3), 1) * (lay.n_dev * n_par // 2))
    code_ref[:, 0:lay.list_len] = (place * 512 + kind_ref[...]).T
    codes = code_ref[pl.ds(pl.multiple_of(ang_ref[0] * n_par, n_par), n_par), 0:lay.list_len]
    n_ask = cols_ref.shape[1]
    asks = jnp.concatenate([cols_ref[...], jnp.zeros((1, 128 - n_ask), jnp.int32)], axis=1)
    asks = jnp.broadcast_to(asks, (8, 128)).T[:, 0:1]
    asks = [asks[b:b + n_par] for b in range(0, n_ask, n_par)]

    def radiate_tile(i, carry):
        rad_piece(i).wait()

        @pl.when(i + 1 < n_interp)
        def _():
            interp_piece(i + 1).start()

        at = pl.ds(pl.multiple_of(i * TILE, TILE), TILE)
        rr_high, rr_low = halves(rad_ref[0, at, :])
        ri_high, ri_low = halves(rad_ref[1, at, :])
        radiated = (dot_nt(left, rr_high) + dot_nt(left, rr_low)
                    + dot_nt(right, ri_high) + dot_nt(right, ri_low))
        high, low = halves(radiated)
        high_ref[:, at] = high
        low_ref[:, at] = low
        return carry

    lax.fori_loop(0, n_rad, radiate_tile, 0)

    def interp_tile(i, carry):
        interp_piece(i).wait()

        @pl.when(i + 1 + n_rad < n_interp)
        def _():
            interp_piece(i + 1 + n_rad).start()

        at = pl.ds(pl.multiple_of(i * ROWS, ROWS), ROWS)
        in_high, in_low = halves(interp_ref[at, :])
        children = (dot_nt(high_ref[...], in_high) + dot_nt(high_ref[...], in_low)
                    + dot_nt(low_ref[...], in_high))
        re_sum = im_sum = None
        for t in range(8):
            c = cos_ref[t:t + 1, at]
            s = sin_ref[t:t + 1, at]
            re = children[t * n_par:(t + 1) * n_par]
            im = children[count + t * n_par:count + (t + 1) * n_par]
            re_t = c * re - s * im
            im_t = c * im + s * re
            re_sum = re_t if t == 0 else re_sum + re_t
            im_sum = im_t if t == 0 else im_sum + im_t
        par_ref[0, :, at] = re_sum
        par_ref[1, :, at] = im_sum
        return carry

    lax.fori_loop(0, n_interp, interp_tile, 0)

    largest = jnp.max(jnp.maximum(jnp.abs(par_ref[0]), jnp.abs(par_ref[1])), axis=1, keepdims=True)
    eighths = exponent(largest)
    words = pack(par_ref[0], par_ref[1], scale_of(eighths))
    notes = [eighths.astype(jnp.int32) + BIAS] + asks
    notes.append(jnp.zeros((n_par, lay.list_len - len(notes)), jnp.int32))
    notes = codes + jnp.left_shift(jnp.concatenate(notes, axis=1), CODE_BITS)
    gap = [jnp.zeros((8, NOTES - lay.own), jnp.int32)] if lay.own < NOTES else []
    for dest in range(lay.n_dev):
        at = slice(lay.first(dest), lay.first(dest) + lay.own)
        out_ref[dest] = jnp.concatenate(
            [words[0:8, at], *gap, notes[0:8], words[8:16, at], *gap, notes[8:16]], axis=1)


def forward(lay, ang, current, radiate, interp, phase, sources, types, cols):
    count = current.shape[1]
    k_up, k_leaf = interp.shape
    n_par = count // 8
    return pl.pallas_call(
        functools.partial(forward_kernel, lay),
        in_specs=[SMEM] + [HBM] * 7,
        out_specs=[VMEM] * 3,
        out_shape=[
            jax.ShapeDtypeStruct((lay.n_dev, 8, 128), jnp.int32),
            jax.ShapeDtypeStruct(phase.shape, F32),
            jax.ShapeDtypeStruct(phase.shape, F32),
        ],
        scratch_shapes=[
            pltpu.VMEM(current.shape, BF16),
            pltpu.VMEM(phase.shape, F32),
            pltpu.VMEM(sources.shape[::-1], jnp.int32),
            pltpu.VMEM(types.shape[::-1], jnp.int32),
            pltpu.VMEM(cols.shape, jnp.int32),
            pltpu.VMEM(radiate.shape, F32),
            pltpu.VMEM(interp.shape, F32),
            pltpu.VMEM((2 * count, k_leaf), BF16),
            pltpu.VMEM((2 * count, k_leaf), BF16),
            pltpu.VMEM((2, n_par, k_up), F32),
            pltpu.VMEM((sources.shape[0], 128), jnp.int32),
            pltpu.SemaphoreType.DMA((5,)),
            pltpu.SemaphoreType.DMA((k_leaf // TILE,)),
            pltpu.SemaphoreType.DMA((k_up // ROWS,)),
        ],
        compiler_params=pltpu.CompilerParams(vmem_limit_bytes=VMEM_LIMIT),
        cost_estimate=pl.CostEstimate(flops=3 * 10**9, bytes_accessed=9 * 10**6, transcendentals=0),
        name="forward",
    )(ang, *map(in_hbm, (current, phase, sources.T, types.T, cols, radiate, interp)))


def translate_kernel(lay, got_ref, table_ref, out_ref, x_ref, t_ref, acc_ref):
    n_par = 2 * got_ref.shape[0]
    side = n_par // 2
    span = 2 * lay.pad
    n_pad = table_ref.shape[1]
    got = got_ref[...].T
    codes = []
    for h in range(2):
        words = got[HALF * h:HALF * h + lay.pad]
        codes.append(got[HALF * h + NOTES:HALF * h + NOTES + lay.list_len])
        scale = scale_of((note(codes[h][0:1]) - BIAS).astype(F32))
        for part, value in enumerate(unpack(words, scale)):
            high, low = halves(value)
            at = lay.pad * part
            x_ref[at:at + lay.pad, side * h:side * h + side] = high
            x_ref[span + at:span + at + lay.pad, side * h:side * h + side] = low
    codes = jnp.bitwise_and(jnp.concatenate(codes, axis=1), (1 << CODE_BITS) - 1)
    high, low = halves(table_ref[...])
    t_ref[0:span] = high
    t_ref[span:2 * span] = low
    width = min(512, n_par)
    rows_src = iota((n_par, width), 0)
    rows_kind = iota((n_pad, width), 0)
    for p in range(0, n_par, width):
        at = slice(p, p + width)
        re_sum = im_sum = 0.0
        for m in range(lay.list_len):
            code = codes[m:m + 1, at]
            source = jnp.right_shift(code, 9)
            kind = jnp.bitwise_and(code, 511)
            pick = (rows_src == source).astype(BF16)
            both = dot_nn(x_ref[...], pick)
            chosen = both[0:span] + both[span:2 * span]
            pick = (rows_kind == kind).astype(BF16)
            both = dot_nn(t_ref[...], pick)
            factor = both[0:span] + both[span:2 * span]
            fr, fi = factor[0:lay.pad], factor[lay.pad:span]
            cr, ci = chosen[0:lay.pad], chosen[lay.pad:span]
            re_sum = re_sum + (fr * cr - fi * ci)
            im_sum = im_sum + (fr * ci + fi * cr)
        largest = jnp.maximum(jnp.max(jnp.abs(re_sum), axis=0, keepdims=True),
                              jnp.max(jnp.abs(im_sum), axis=0, keepdims=True))
        eighths = exponent(largest)
        acc_ref[0:lay.pad, at] = pack(re_sum, im_sum, scale_of(eighths))
        acc_ref[NOTES:NOTES + 8, at] = jnp.broadcast_to(eighths, (8, width)).astype(jnp.int32)
    for h in range(2):
        out_ref[:, HALF * h:HALF * h + HALF] = acc_ref[:, side * h:side * h + side].T


def translate_far(lay, got, table):
    n_par = 2 * got.shape[0]
    span = 2 * lay.pad
    return pl.pallas_call(
        functools.partial(translate_kernel, lay),
        in_specs=[VMEM] * 2,
        out_specs=VMEM,
        out_shape=jax.ShapeDtypeStruct(got.shape, jnp.int32),
        scratch_shapes=[
            pltpu.VMEM((2 * span, n_par), BF16),
            pltpu.VMEM((2 * span, table.shape[1]), BF16),
            pltpu.VMEM((HALF, n_par), jnp.int32),
        ],
        compiler_params=pltpu.CompilerParams(vmem_limit_bytes=VMEM_LIMIT),
        cost_estimate=pl.CostEstimate(flops=2 * 10**9, bytes_accessed=10**6, transcendentals=0),
        name="translate_far",
    )(got, table)


def backward_kernel(lay, got_ref, cos_ref, sin_ref, near_ref, interp_hbm, rec_hbm, out_ref,
                    interp_ref, rec_ref, inc_ref, high_ref, low_ref, leaf_ref, interp_sems, rec_sems):
    interp_piece = piece(interp_hbm, interp_ref, interp_sems, 0, ROWS)
    rec_piece = piece(rec_hbm, rec_ref, rec_sems, 1, TILE)
    n_interp, n_rec = interp_sems.shape[0], rec_sems.shape[0]
    for i in range(3):
        interp_piece(i).start()
    count = near_ref.shape[1]
    n_par = count // 8

    for dest in range(lay.n_dev):
        words = got_ref[dest]
        j = lay.first(dest)
        for h in range(2):
            eighths = words[:, HALF * h + NOTES:HALF * h + NOTES + 1].astype(F32)
            values = unpack(words[:, HALF * h:HALF * h + lay.own], scale_of(eighths))
            for part in range(2):
                inc_ref[part, 8 * h:8 * h + 8, j:j + lay.own] = values[part]
    c = cos_ref[...]
    s = sin_ref[...]
    for p in range(0, n_par, 2):
        res, ims = [], []
        for q in (p, p + 1):
            re = inc_ref[0, q:q + 1, :]
            im = inc_ref[1, q:q + 1, :]
            res.append(c * re + s * im)
            ims.append(c * im - s * re)
        high, low = halves(jnp.concatenate(res, axis=0))
        high_ref[8 * p:8 * p + 16] = high
        low_ref[8 * p:8 * p + 16] = low
        high, low = halves(jnp.concatenate(ims, axis=0))
        high_ref[count + 8 * p:count + 8 * p + 16] = high
        low_ref[count + 8 * p:count + 8 * p + 16] = low

    leaf_ref[...] = jnp.zeros_like(leaf_ref)

    def leaf_tile(i, carry):
        interp_piece(i).wait()

        @pl.when(i + 3 < n_interp)
        def _():
            interp_piece(i + 3).start()

        @pl.when(i + 3 >= n_interp)
        def _():
            @pl.when(i + 3 - n_interp < n_rec)
            def _():
                rec_piece(i + 3 - n_interp).start()

        at = pl.ds(pl.multiple_of(i * ROWS, ROWS), ROWS)
        in_high, in_low = halves(interp_ref[at, :])
        leaf_ref[...] += (dot_nn(high_ref[:, at], in_high) + dot_nn(high_ref[:, at], in_low)
                          + dot_nn(low_ref[:, at], in_high))
        return carry

    lax.fori_loop(0, n_interp, leaf_tile, 0)
    for i in range(n_rec):
        rec_piece(i).wait()
    leaf_high, leaf_low = halves(leaf_ref[...])
    by = []
    for part in range(2):
        rec_high, rec_low = halves(rec_ref[part])
        by.append(dot_nn(leaf_high, rec_high) + dot_nn(leaf_high, rec_low) + dot_nn(leaf_low, rec_high))
    re_sum = near_ref[0] + (by[0][0:count] - by[1][count:2 * count])
    im_sum = near_ref[1] + (by[1][0:count] + by[0][count:2 * count])
    out_ref[0] = re_sum
    out_ref[1] = im_sum


def backward(lay, got, interp, receive, cosine, sine, near):
    count = near.shape[1]
    n_par = count // 8
    k_up, k_leaf = interp.shape
    unk = receive.shape[2]
    return pl.pallas_call(
        functools.partial(backward_kernel, lay),
        in_specs=[VMEM] * 4 + [HBM] * 2,
        out_specs=VMEM,
        out_shape=jax.ShapeDtypeStruct((2, count, unk), F32),
        scratch_shapes=[
            pltpu.VMEM(interp.shape, F32),
            pltpu.VMEM(receive.shape, F32),
            pltpu.VMEM((2, n_par, k_up), F32),
            pltpu.VMEM((2 * count, k_up), BF16),
            pltpu.VMEM((2 * count, k_up), BF16),
            pltpu.VMEM((2 * count, k_leaf), F32),
            pltpu.SemaphoreType.DMA((k_up // ROWS,)),
            pltpu.SemaphoreType.DMA((k_leaf // TILE,)),
        ],
        compiler_params=pltpu.CompilerParams(vmem_limit_bytes=VMEM_LIMIT),
        cost_estimate=pl.CostEstimate(flops=3 * 10**9, bytes_accessed=9 * 10**6, transcendentals=0),
        name="backward",
    )(pltpu.with_memory_space_constraint(got, pltpu.VMEM), cosine, sine, near, in_hbm(interp), in_hbm(receive))


def pick_kernel(lay, n_block, me_ref, got_ref, cur_ref, *out_refs):
    count = cur_ref.shape[1]
    first = me_ref[0]
    ang = me_ref[1]
    for mask, out_ref in enumerate(out_refs):
        dest = first + jnp.bitwise_xor(ang, mask)
        notes = note(got_ref[dest])
        marks = []
        for field in range(1, 1 + -(-n_block // 16)):
            for h in range(2):
                lane = HALF * h + NOTES + field
                marks.append((iota((8, count), 1) == notes[:, lane:lane + 1] - ang * count).astype(F32))
        mark = jnp.concatenate(marks, axis=0).astype(BF16)
        both = [dot_nn(mark, cur_ref[part])[0:n_block] for part in range(2)]
        out_ref[...] = jnp.concatenate(both, axis=0).astype(BF16)


def pick_columns(lay, n_block, me, got, current):
    unk = current.shape[2]
    one = jax.ShapeDtypeStruct((2 * n_block, unk), BF16)
    return pl.pallas_call(
        functools.partial(pick_kernel, lay, n_block),
        in_specs=[SMEM, VMEM, VMEM],
        out_specs=[VMEM] * lay.n_ang,
        out_shape=[one] * lay.n_ang,
        compiler_params=pltpu.CompilerParams(vmem_limit_bytes=VMEM_LIMIT),
        cost_estimate=pl.CostEstimate(flops=10**8, bytes_accessed=10**6, transcendentals=0),
        name="pick_columns",
    )(me, got, current)


def swap(picked, n_ang):
    half = [picked[mask] for mask in range(0, n_ang, 2)]
    sent = jnp.stack([picked[mask] for mask in range(1, n_ang, 2)])
    got = lax.ppermute(sent, "ang", [(i, i ^ 1) for i in range(n_ang)])
    return [one + got[k] for k, one in enumerate(half)]


def answers(half, n_ang):
    return [half[0]] + [
        lax.ppermute(half[k], "ang", [(i, i ^ (2 * k)) for i in range(n_ang)]) for k in range(1, len(half))
    ]


def near_kernel(n_term, *refs):
    rows_ref, terms, (blocks_hbm, out_ref, blocks_ref, wide_ref, own_ref, sems) = (
        refs[0], refs[1:1 + n_term], refs[1 + n_term:])
    n_block, _, unk, _ = blocks_ref.shape
    here = n_block // sems.shape[0]

    block_piece = piece(blocks_hbm, blocks_ref, sems, 0, here)
    n_piece = sems.shape[0]
    for i in range(3):
        block_piece(i).start()
    total = terms[0][...].astype(F32)
    for term in terms[1:]:
        total = total + term[...].astype(F32)
    gap = jnp.zeros((64 - n_block, unk), F32)
    wide_ref[...] = jnp.concatenate([total[0:n_block], gap, total[n_block:], gap], axis=0).astype(BF16)
    lane = iota((2 * unk, 128), 1) % 64
    own_ref[...] = jnp.zeros_like(own_ref)

    def some_blocks(i, carry):
        block_piece(i).wait()

        @pl.when(i + 3 < n_piece)
        def _():
            block_piece(i + 3).start()

        rows = blocks_ref[pl.ds(i * here, here)].reshape(here * 2 * unk, unk)
        products = dot_nt(rows, wide_ref[...])
        own = own_ref[...]
        for k in range(here):
            own = jnp.where(lane == i * here + k, products[2 * unk * k:2 * unk * (k + 1)], own)
        own_ref[...] = own
        return carry

    lax.fori_loop(0, n_piece, some_blocks, 0)

    by_block = own_ref[...].T
    by_re, by_im = by_block[:, 0:unk], by_block[:, unk:2 * unk]
    re = by_re[0:n_block] - by_im[64:64 + n_block]
    im = by_re[64:64 + n_block] + by_im[0:n_block]
    count = out_ref.shape[1]
    mark = (iota((count, n_block), 0) == rows_ref[...]).astype(BF16)
    for part, value in ((0, re), (1, im)):
        high, low = halves(value)
        out_ref[part] = dot_nn(mark, high) + dot_nn(mark, low)


def near_field(rows, terms, blocks, count):
    n_block, _, unk, _ = blocks.shape
    here = 8
    return pl.pallas_call(
        functools.partial(near_kernel, len(terms)),
        in_specs=[VMEM] * (1 + len(terms)) + [HBM],
        out_specs=VMEM,
        out_shape=jax.ShapeDtypeStruct((2, count, unk), F32),
        scratch_shapes=[
            pltpu.VMEM(blocks.shape, BF16),
            pltpu.VMEM((128, unk), BF16),
            pltpu.VMEM((2 * unk, 128), F32),
            pltpu.SemaphoreType.DMA((n_block // here,)),
        ],
        compiler_params=pltpu.CompilerParams(vmem_limit_bytes=VMEM_LIMIT),
        cost_estimate=pl.CostEstimate(flops=2 * 10**11, bytes_accessed=12 * 10**6, transcendentals=0),
        name="near_field",
    )(rows, *terms, in_hbm(blocks))


def on_device(n_grp, n_ang, current, near_blocks, near_rows, near_cols, radiate, receive, interp,
              shift_phase, translate, far_sources, far_types):
    count, unk = current.shape[1:]
    n_par = count // 8
    n_block = near_blocks.shape[0]
    k_up = interp.shape[0]
    n_kind = translate.shape[1]
    lay = Layout(n_grp, n_ang, k_up, far_sources.shape[1])
    grp = lax.axis_index("grp")
    ang = lax.axis_index("ang")
    axes = ("grp", "ang")

    message, cosine, sine = forward(
        lay, ang[None], current, radiate, interp, shift_phase, far_sources, far_types, near_cols[None])
    got = lax.all_to_all(message, axes, 0, 0)
    half = swap(pick_columns(lay, n_block, jnp.stack([grp * n_ang, ang]), got, current), n_ang)

    table = lax.dynamic_slice_in_dim(translate, grp * lay.own, lay.own, 2)
    kind_pad = -(-n_kind // 128) * 128
    table = jnp.pad(table, ((0, 0), (0, kind_pad - n_kind), (0, lay.pad - lay.own)))
    table = jnp.transpose(table, (0, 2, 1)).reshape(2 * lay.pad, kind_pad)

    incoming = translate_far(lay, got.reshape(lay.n_dev * 8, 128), table)
    incoming, half = lax.optimization_barrier((incoming, half))
    near = near_field(near_rows[None], answers(half, n_ang), near_blocks, count)
    returned = lax.all_to_all(incoming.reshape(lay.n_dev, 8, 128), axes, 0, 0)

    return backward(lay, returned, interp, receive, cosine, sine, near)


def solution(mesh):
    both = ("grp", "ang")
    in_specs = (
        P(None, both, None),
        P(both, None, None, None),
        P(both),
        P(both),
        P(),
        P(),
        P(),
        P(),
        P(None, None, "ang"),
        P("grp", None),
        P("grp", None),
    )
    run = functools.partial(on_device, mesh.shape["grp"], mesh.shape["ang"])
    return jax.shard_map(run, mesh=mesh, in_specs=in_specs, out_specs=P(None, both, None), check_vma=False)
```

```python
import functools
import jax
import jax.numpy as jnp
from jax import lax
from jax.experimental import pallas as pl
from jax.experimental.pallas import tpu as pltpu
from jax.sharding import PartitionSpec as P

F32 = jnp.float32
BF16 = jnp.bfloat16
VMEM_LIMIT = 24 << 20
HBM = pl.BlockSpec(memory_space=pltpu.HBM)
VMEM = pl.BlockSpec(memory_space=pltpu.VMEM)
SMEM = pl.BlockSpec(memory_space=pltpu.SMEM)
TILE = 512
ROWS = 512


def halves(x):
    high = x.astype(BF16)
    return high, (x - high.astype(F32)).astype(BF16)


def dot_nt(a, b):
    return lax.dot_general(a, b, (((1,), (1,)), ((), ())), preferred_element_type=F32)


def dot_nn(a, b):
    return lax.dot_general(a, b, (((1,), (0,)), ((), ())), preferred_element_type=F32)


def in_hbm(x):
    return pltpu.with_memory_space_constraint(x, pltpu.HBM)


def iota(shape, dim):
    return lax.broadcasted_iota(jnp.int32, shape, dim)


class Layout:
    def __init__(self, n_grp, n_ang, k_up, list_len):
        self.n_grp, self.n_ang = n_grp, n_ang
        self.n_dev = n_grp * n_ang
        self.own = k_up // self.n_dev
        self.pad = -(-self.own // 8) * 8
        self.list_len = list_len

    def first(self, dest):
        grp, ang = divmod(dest, self.n_ang)
        return (ang * self.n_grp + grp) * self.own


HALF = 64
NOTES = 48
CODE_BITS = 20
BIAS = 2048


def exponent(largest):
    return jnp.ceil(8.0 * jnp.log2(jnp.maximum(largest, 1e-30)))


def scale_of(eighths):
    return jnp.exp2(eighths * 0.125)


def pack(re, im, scale):
    def grid(x):
        return jnp.clip(jnp.round(x * (32767.0 / scale)), -32767.0, 32767.0).astype(jnp.int32)
    return jnp.bitwise_or(jnp.left_shift(grid(re), 16), jnp.bitwise_and(grid(im), 65535))


def unpack(words, scale):
    step = scale * (1.0 / 32767.0)
    re = jnp.right_shift(words, 16).astype(F32) * step
    im = jnp.right_shift(jnp.left_shift(words, 16), 16).astype(F32) * step
    return re, im


def note(word):
    return lax.shift_right_logical(word, CODE_BITS)


def piece(source, target, sems, dim, size):
    def at(i):
        index = (slice(None),) * dim + (pl.ds(pl.multiple_of(i * size, size), size),)
        return pltpu.make_async_copy(source.at[index], target.at[index], sems.at[i])
    return at


def forward_kernel(lay, ang_ref, cur_hbm, phase_hbm, src_hbm, kind_hbm, cols_hbm, rad_hbm, interp_hbm, out_ref, cos_ref,
                   sin_ref, cur_ref, phase_ref, src_ref, kind_ref, cols_ref, rad_ref, interp_ref, high_ref, low_ref,
                   par_ref, code_ref, small_sems, rad_sems, interp_sems):
    small = [
        pltpu.make_async_copy(source, target, small_sems.at[i])
        for i, (source, target) in enumerate([
            (cur_hbm, cur_ref), (phase_hbm, phase_ref), (src_hbm, src_ref), (kind_hbm, kind_ref),
            (cols_hbm, cols_ref)])
    ]
    for copy in small:
        copy.start()
    rad_piece = piece(rad_hbm, rad_ref, rad_sems, 1, TILE)
    interp_piece = piece(interp_hbm, interp_ref, interp_sems, 0, ROWS)
    n_rad, n_interp = rad_sems.shape[0], interp_sems.shape[0]
    for i in range(n_rad):
        rad_piece(i).start()
    interp_piece(0).start()
    for copy in small:
        copy.wait()
    count = cur_ref.shape[1]
    n_par = count // 8
    k_up, k_leaf = interp_ref.shape

    row = iota((count, count), 0)
    col = iota((count, count), 1)
    order = (col == (row % n_par) * 8 + row // n_par).astype(BF16)
    cur_re = dot_nn(order, cur_ref[0]).astype(BF16)
    cur_im = dot_nn(order, cur_ref[1]).astype(BF16)
    left = jnp.concatenate([cur_re, cur_im], axis=0)
    right = jnp.concatenate([-cur_im, cur_re], axis=0)
    cos_ref[...] = jnp.cos(phase_ref[...])
    sin_ref[...] = jnp.sin(phase_ref[...])

    src = src_ref[...]
    place = (jnp.left_shift(jnp.right_shift(src, 4), 3) + jnp.bitwise_and(src, 7)
             + jnp.bitwise_and(jnp.right_shift(src, 3), 1) * (lay.n_dev * n_par // 2))
    code_ref[:, 0:lay.list_len] = (place * 512 + kind_ref[...]).T
    codes = code_ref[pl.ds(pl.multiple_of(ang_ref[0] * n_par, n_par), n_par), 0:lay.list_len]
    n_ask = cols_ref.shape[1]
    asks = jnp.concatenate([cols_ref[...], jnp.zeros((1, 128 - n_ask), jnp.int32)], axis=1)
    asks = jnp.broadcast_to(asks, (8, 128)).T[:, 0:1]
    asks = [asks[b:b + n_par] for b in range(0, n_ask, n_par)]

    def radiate_tile(i, carry):
        rad_piece(i).wait()

        @pl.when(i + 1 < n_interp)
        def _():
            interp_piece(i + 1).start()

        at = pl.ds(pl.multiple_of(i * TILE, TILE), TILE)
        rr_high, rr_low = halves(rad_ref[0, at, :])
        ri_high, ri_low = halves(rad_ref[1, at, :])
        radiated = (dot_nt(left, rr_high) + dot_nt(left, rr_low)
                    + dot_nt(right, ri_high) + dot_nt(right, ri_low))
        high, low = halves(radiated)
        high_ref[:, at] = high
        low_ref[:, at] = low
        return carry

    lax.fori_loop(0, n_rad, radiate_tile, 0)

    def interp_tile(i, carry):
        interp_piece(i).wait()

        @pl.when(i + 1 + n_rad < n_interp)
        def _():
            interp_piece(i + 1 + n_rad).start()

        at = pl.ds(pl.multiple_of(i * ROWS, ROWS), ROWS)
        in_high, in_low = halves(interp_ref[at, :])
        children = (dot_nt(high_ref[...], in_high) + dot_nt(high_ref[...], in_low)
                    + dot_nt(low_ref[...], in_high))
        re_sum = im_sum = None
        for t in range(8):
            c = cos_ref[t:t + 1, at]
            s = sin_ref[t:t + 1, at]
            re = children[t * n_par:(t + 1) * n_par]
            im = children[count + t * n_par:count + (t + 1) * n_par]
            re_t = c * re - s * im
            im_t = c * im + s * re
            re_sum = re_t if t == 0 else re_sum + re_t
            im_sum = im_t if t == 0 else im_sum + im_t
        par_ref[0, :, at] = re_sum
        par_ref[1, :, at] = im_sum
        return carry

    lax.fori_loop(0, n_interp, interp_tile, 0)

    largest = jnp.max(jnp.maximum(jnp.abs(par_ref[0]), jnp.abs(par_ref[1])), axis=1, keepdims=True)
    eighths = exponent(largest)
    words = pack(par_ref[0], par_ref[1], scale_of(eighths))
    notes = [eighths.astype(jnp.int32) + BIAS] + asks
    notes.append(jnp.zeros((n_par, lay.list_len - len(notes)), jnp.int32))
    notes = codes + jnp.left_shift(jnp.concatenate(notes, axis=1), CODE_BITS)
    gap = [jnp.zeros((8, NOTES - lay.own), jnp.int32)] if lay.own < NOTES else []
    for dest in range(lay.n_dev):
        at = slice(lay.first(dest), lay.first(dest) + lay.own)
        out_ref[dest] = jnp.concatenate(
            [words[0:8, at], *gap, notes[0:8], words[8:16, at], *gap, notes[8:16]], axis=1)


def forward(lay, ang, current, radiate, interp, phase, sources, types, cols):
    count = current.shape[1]
    k_up, k_leaf = interp.shape
    n_par = count // 8
    return pl.pallas_call(
        functools.partial(forward_kernel, lay),
        in_specs=[SMEM] + [HBM] * 7,
        out_specs=[VMEM] * 3,
        out_shape=[
            jax.ShapeDtypeStruct((lay.n_dev, 8, 128), jnp.int32),
            jax.ShapeDtypeStruct(phase.shape, F32),
            jax.ShapeDtypeStruct(phase.shape, F32),
        ],
        scratch_shapes=[
            pltpu.VMEM(current.shape, BF16),
            pltpu.VMEM(phase.shape, F32),
            pltpu.VMEM(sources.shape[::-1], jnp.int32),
            pltpu.VMEM(types.shape[::-1], jnp.int32),
            pltpu.VMEM(cols.shape, jnp.int32),
            pltpu.VMEM(radiate.shape, F32),
            pltpu.VMEM(interp.shape, F32),
            pltpu.VMEM((2 * count, k_leaf), BF16),
            pltpu.VMEM((2 * count, k_leaf), BF16),
            pltpu.VMEM((2, n_par, k_up), F32),
            pltpu.VMEM((sources.shape[0], 128), jnp.int32),
            pltpu.SemaphoreType.DMA((5,)),
            pltpu.SemaphoreType.DMA((k_leaf // TILE,)),
            pltpu.SemaphoreType.DMA((k_up // ROWS,)),
        ],
        compiler_params=pltpu.CompilerParams(vmem_limit_bytes=VMEM_LIMIT),
        cost_estimate=pl.CostEstimate(flops=3 * 10**9, bytes_accessed=9 * 10**6, transcendentals=0),
        name="forward",
    )(ang, *map(in_hbm, (current, phase, sources.T, types.T, cols, radiate, interp)))


def translate_kernel(lay, got_ref, table_ref, out_ref, x_ref, t_ref, acc_ref):
    n_par = 2 * got_ref.shape[0]
    side = n_par // 2
    span = 2 * lay.pad
    n_pad = table_ref.shape[1]
    got = got_ref[...].T
    codes = []
    for h in range(2):
        words = got[HALF * h:HALF * h + lay.pad]
        codes.append(got[HALF * h + NOTES:HALF * h + NOTES + lay.list_len])
        scale = scale_of((note(codes[h][0:1]) - BIAS).astype(F32))
        for part, value in enumerate(unpack(words, scale)):
            high, low = halves(value)
            at = lay.pad * part
            x_ref[at:at + lay.pad, side * h:side * h + side] = high
            x_ref[span + at:span + at + lay.pad, side * h:side * h + side] = low
    codes = jnp.bitwise_and(jnp.concatenate(codes, axis=1), (1 << CODE_BITS) - 1)
    high, low = halves(table_ref[...])
    t_ref[0:span] = high
    t_ref[span:2 * span] = low
    width = min(512, n_par)
    rows_src = iota((n_par, width), 0)
    rows_kind = iota((n_pad, width), 0)
    for p in range(0, n_par, width):
        at = slice(p, p + width)
        re_sum = im_sum = 0.0
        for m in range(lay.list_len):
            code = codes[m:m + 1, at]
            source = jnp.right_shift(code, 9)
            kind = jnp.bitwise_and(code, 511)
            pick = (rows_src == source).astype(BF16)
            both = dot_nn(x_ref[...], pick)
            chosen = both[0:span] + both[span:2 * span]
            pick = (rows_kind == kind).astype(BF16)
            both = dot_nn(t_ref[...], pick)
            factor = both[0:span] + both[span:2 * span]
            fr, fi = factor[0:lay.pad], factor[lay.pad:span]
            cr, ci = chosen[0:lay.pad], chosen[lay.pad:span]
            re_sum = re_sum + (fr * cr - fi * ci)
            im_sum = im_sum + (fr * ci + fi * cr)
        largest = jnp.maximum(jnp.max(jnp.abs(re_sum), axis=0, keepdims=True),
                              jnp.max(jnp.abs(im_sum), axis=0, keepdims=True))
        eighths = exponent(largest)
        acc_ref[0:lay.pad, at] = pack(re_sum, im_sum, scale_of(eighths))
        acc_ref[NOTES:NOTES + 8, at] = jnp.broadcast_to(eighths, (8, width)).astype(jnp.int32)
    for h in range(2):
        out_ref[:, HALF * h:HALF * h + HALF] = acc_ref[:, side * h:side * h + side].T


def translate_far(lay, got, table):
    n_par = 2 * got.shape[0]
    span = 2 * lay.pad
    return pl.pallas_call(
        functools.partial(translate_kernel, lay),
        in_specs=[VMEM] * 2,
        out_specs=VMEM,
        out_shape=jax.ShapeDtypeStruct(got.shape, jnp.int32),
        scratch_shapes=[
            pltpu.VMEM((2 * span, n_par), BF16),
            pltpu.VMEM((2 * span, table.shape[1]), BF16),
            pltpu.VMEM((HALF, n_par), jnp.int32),
        ],
        compiler_params=pltpu.CompilerParams(vmem_limit_bytes=VMEM_LIMIT),
        cost_estimate=pl.CostEstimate(flops=2 * 10**9, bytes_accessed=10**6, transcendentals=0),
        name="translate_far",
    )(got, table)


def backward_kernel(lay, got_ref, cos_ref, sin_ref, near_ref, interp_hbm, rec_hbm, out_ref,
                    interp_ref, rec_ref, inc_ref, high_ref, low_ref, leaf_ref, interp_sems, rec_sems):
    interp_piece = piece(interp_hbm, interp_ref, interp_sems, 0, ROWS)
    rec_piece = piece(rec_hbm, rec_ref, rec_sems, 1, TILE)
    n_interp, n_rec = interp_sems.shape[0], rec_sems.shape[0]
    order = [(interp_piece, i) for i in range(n_interp)] + [(rec_piece, i) for i in range(n_rec)]
    for fetch, i in order[:3]:
        fetch(i).start()
    count = near_ref.shape[1]
    n_par = count // 8

    for dest in range(lay.n_dev):
        words = got_ref[dest]
        j = lay.first(dest)
        for h in range(2):
            eighths = words[:, HALF * h + NOTES:HALF * h + NOTES + 1].astype(F32)
            values = unpack(words[:, HALF * h:HALF * h + lay.own], scale_of(eighths))
            for part in range(2):
                inc_ref[part, 8 * h:8 * h + 8, j:j + lay.own] = values[part]
    c = cos_ref[...]
    s = sin_ref[...]
    for p in range(0, n_par, 2):
        res, ims = [], []
        for q in (p, p + 1):
            re = inc_ref[0, q:q + 1, :]
            im = inc_ref[1, q:q + 1, :]
            res.append(c * re + s * im)
            ims.append(c * im - s * re)
        high, low = halves(jnp.concatenate(res, axis=0))
        high_ref[8 * p:8 * p + 16] = high
        low_ref[8 * p:8 * p + 16] = low
        high, low = halves(jnp.concatenate(ims, axis=0))
        high_ref[count + 8 * p:count + 8 * p + 16] = high
        low_ref[count + 8 * p:count + 8 * p + 16] = low

    leaf_ref[...] = jnp.zeros_like(leaf_ref)

    def leaf_tile(i, carry):
        interp_piece(i).wait()

        for k, (fetch, which) in enumerate(order[3:]):
            @pl.when(i == min(k, n_interp - 1))
            def _():
                fetch(which).start()

        at = pl.ds(pl.multiple_of(i * ROWS, ROWS), ROWS)
        in_high, in_low = halves(interp_ref[at, :])
        leaf_ref[...] += (dot_nn(high_ref[:, at], in_high) + dot_nn(high_ref[:, at], in_low)
                          + dot_nn(low_ref[:, at], in_high))
        return carry

    lax.fori_loop(0, n_interp, leaf_tile, 0)
    for i in range(n_rec):
        rec_piece(i).wait()
    leaf_high, leaf_low = halves(leaf_ref[...])
    by = []
    for part in range(2):
        rec_high, rec_low = halves(rec_ref[part])
        by.append(dot_nn(leaf_high, rec_high) + dot_nn(leaf_high, rec_low) + dot_nn(leaf_low, rec_high))
    re_sum = near_ref[0] + (by[0][0:count] - by[1][count:2 * count])
    im_sum = near_ref[1] + (by[1][0:count] + by[0][count:2 * count])
    out_ref[0] = re_sum
    out_ref[1] = im_sum


def backward(lay, got, interp, receive, cosine, sine, near):
    count = near.shape[1]
    n_par = count // 8
    k_up, k_leaf = interp.shape
    unk = receive.shape[2]
    return pl.pallas_call(
        functools.partial(backward_kernel, lay),
        in_specs=[VMEM] * 4 + [HBM] * 2,
        out_specs=VMEM,
        out_shape=jax.ShapeDtypeStruct((2, count, unk), F32),
        scratch_shapes=[
            pltpu.VMEM(interp.shape, F32),
            pltpu.VMEM(receive.shape, F32),
            pltpu.VMEM((2, n_par, k_up), F32),
            pltpu.VMEM((2 * count, k_up), BF16),
            pltpu.VMEM((2 * count, k_up), BF16),
            pltpu.VMEM((2 * count, k_leaf), F32),
            pltpu.SemaphoreType.DMA((k_up // ROWS,)),
            pltpu.SemaphoreType.DMA((k_leaf // TILE,)),
        ],
        compiler_params=pltpu.CompilerParams(vmem_limit_bytes=VMEM_LIMIT),
        cost_estimate=pl.CostEstimate(flops=3 * 10**9, bytes_accessed=9 * 10**6, transcendentals=0),
        name="backward",
    )(pltpu.with_memory_space_constraint(got, pltpu.VMEM), cosine, sine, near, in_hbm(interp), in_hbm(receive))


def pick_kernel(lay, n_block, me_ref, got_ref, cur_ref, *out_refs):
    count = cur_ref.shape[1]
    first = me_ref[0]
    ang = me_ref[1]
    for mask, out_ref in enumerate(out_refs):
        dest = first + jnp.bitwise_xor(ang, mask)
        notes = note(got_ref[dest])
        marks = []
        for field in range(1, 1 + -(-n_block // 16)):
            for h in range(2):
                lane = HALF * h + NOTES + field
                marks.append((iota((8, count), 1) == notes[:, lane:lane + 1] - ang * count).astype(F32))
        mark = jnp.concatenate(marks, axis=0).astype(BF16)
        both = [dot_nn(mark, cur_ref[part])[0:n_block] for part in range(2)]
        out_ref[...] = jnp.concatenate(both, axis=0).astype(BF16)


def pick_columns(lay, n_block, me, got, current):
    unk = current.shape[2]
    one = jax.ShapeDtypeStruct((2 * n_block, unk), BF16)
    return pl.pallas_call(
        functools.partial(pick_kernel, lay, n_block),
        in_specs=[SMEM, VMEM, VMEM],
        out_specs=[VMEM] * lay.n_ang,
        out_shape=[one] * lay.n_ang,
        compiler_params=pltpu.CompilerParams(vmem_limit_bytes=VMEM_LIMIT),
        cost_estimate=pl.CostEstimate(flops=10**8, bytes_accessed=10**6, transcendentals=0),
        name="pick_columns",
    )(me, got, current)


def swap(picked, n_ang):
    half = [picked[mask] for mask in range(0, n_ang, 2)]
    sent = jnp.stack([picked[mask] for mask in range(1, n_ang, 2)])
    got = lax.ppermute(sent, "ang", [(i, i ^ 1) for i in range(n_ang)])
    return [one + got[k] for k, one in enumerate(half)]


def answers(half, n_ang):
    return [half[0]] + [
        lax.ppermute(half[k], "ang", [(i, i ^ (2 * k)) for i in range(n_ang)]) for k in range(1, len(half))
    ]


def near_kernel(n_term, *refs):
    rows_ref, terms, (blocks_hbm, out_ref, blocks_ref, wide_ref, own_ref, sems) = (
        refs[0], refs[1:1 + n_term], refs[1 + n_term:])
    n_block, _, unk, _ = blocks_ref.shape
    here = n_block // sems.shape[0]

    block_piece = piece(blocks_hbm, blocks_ref, sems, 0, here)
    n_piece = sems.shape[0]
    for i in range(3):
        block_piece(i).start()
    total = terms[0][...].astype(F32)
    for term in terms[1:]:
        total = total + term[...].astype(F32)
    gap = jnp.zeros((64 - n_block, unk), F32)
    wide_ref[...] = jnp.concatenate([total[0:n_block], gap, total[n_block:], gap], axis=0).astype(BF16)
    lane = iota((2 * unk, 128), 1) % 64
    own_ref[...] = jnp.zeros_like(own_ref)

    def some_blocks(i, carry):
        block_piece(i).wait()

        @pl.when(i + 3 < n_piece)
        def _():
            block_piece(i + 3).start()

        rows = blocks_ref[pl.ds(i * here, here)].reshape(here * 2 * unk, unk)
        products = dot_nt(rows, wide_ref[...])
        own = own_ref[...]
        for k in range(here):
            own = jnp.where(lane == i * here + k, products[2 * unk * k:2 * unk * (k + 1)], own)
        own_ref[...] = own
        return carry

    lax.fori_loop(0, n_piece, some_blocks, 0)

    by_block = own_ref[...].T
    by_re, by_im = by_block[:, 0:unk], by_block[:, unk:2 * unk]
    re = by_re[0:n_block] - by_im[64:64 + n_block]
    im = by_re[64:64 + n_block] + by_im[0:n_block]
    count = out_ref.shape[1]
    mark = (iota((count, n_block), 0) == rows_ref[...]).astype(BF16)
    for part, value in ((0, re), (1, im)):
        high, low = halves(value)
        out_ref[part] = dot_nn(mark, high) + dot_nn(mark, low)


def near_field(rows, terms, blocks, count):
    n_block, _, unk, _ = blocks.shape
    here = 8
    return pl.pallas_call(
        functools.partial(near_kernel, len(terms)),
        in_specs=[VMEM] * (1 + len(terms)) + [HBM],
        out_specs=VMEM,
        out_shape=jax.ShapeDtypeStruct((2, count, unk), F32),
        scratch_shapes=[
            pltpu.VMEM(blocks.shape, BF16),
            pltpu.VMEM((128, unk), BF16),
            pltpu.VMEM((2 * unk, 128), F32),
            pltpu.SemaphoreType.DMA((n_block // here,)),
        ],
        compiler_params=pltpu.CompilerParams(vmem_limit_bytes=VMEM_LIMIT),
        cost_estimate=pl.CostEstimate(flops=2 * 10**10, bytes_accessed=12 * 10**6, transcendentals=0),
        name="near_field",
    )(rows, *terms, in_hbm(blocks))


def on_device(n_grp, n_ang, current, near_blocks, near_rows, near_cols, radiate, receive, interp,
              shift_phase, translate, far_sources, far_types):
    count, unk = current.shape[1:]
    n_par = count // 8
    n_block = near_blocks.shape[0]
    k_up = interp.shape[0]
    n_kind = translate.shape[1]
    lay = Layout(n_grp, n_ang, k_up, far_sources.shape[1])
    grp = lax.axis_index("grp")
    ang = lax.axis_index("ang")
    axes = ("grp", "ang")

    message, cosine, sine = forward(
        lay, ang[None], current, radiate, interp, shift_phase, far_sources, far_types, near_cols[None])
    got = lax.all_to_all(message, axes, 0, 0)
    half = swap(pick_columns(lay, n_block, jnp.stack([grp * n_ang, ang]), got, current), n_ang)

    table = lax.dynamic_slice_in_dim(translate, grp * lay.own, lay.own, 2)
    kind_pad = -(-n_kind // 128) * 128
    table = jnp.pad(table, ((0, 0), (0, kind_pad - n_kind), (0, lay.pad - lay.own)))
    table = jnp.transpose(table, (0, 2, 1)).reshape(2 * lay.pad, kind_pad)

    incoming = translate_far(lay, got.reshape(lay.n_dev * 8, 128), table)
    incoming, half = lax.optimization_barrier((incoming, half))
    near = near_field(near_rows[None], answers(half, n_ang), near_blocks, count)
    returned = lax.all_to_all(incoming.reshape(lay.n_dev, 8, 128), axes, 0, 0)

    return backward(lay, returned, interp, receive, cosine, sine, near)


def solution(mesh):
    both = ("grp", "ang")
    in_specs = (
        P(None, both, None),
        P(both, None, None, None),
        P(both),
        P(both),
        P(),
        P(),
        P(),
        P(),
        P(None, None, "ang"),
        P("grp", None),
        P("grp", None),
    )
    run = functools.partial(on_device, mesh.shape["grp"], mesh.shape["ang"])
    return jax.shard_map(run, mesh=mesh, in_specs=in_specs, out_specs=P(None, both, None), check_vma=False)
```

```python
import functools
import jax
import jax.numpy as jnp
from jax import lax
from jax.experimental import pallas as pl
from jax.experimental.pallas import tpu as pltpu
from jax.sharding import PartitionSpec as P

F32 = jnp.float32
BF16 = jnp.bfloat16
VMEM_LIMIT = 24 << 20
HBM = pl.BlockSpec(memory_space=pltpu.HBM)
VMEM = pl.BlockSpec(memory_space=pltpu.VMEM)
SMEM = pl.BlockSpec(memory_space=pltpu.SMEM)
TILE = 512
ROWS = 512


def halves(x):
    high = x.astype(BF16)
    return high, (x - high.astype(F32)).astype(BF16)


def dot_nt(a, b):
    return lax.dot_general(a, b, (((1,), (1,)), ((), ())), preferred_element_type=F32)


def dot_nn(a, b):
    return lax.dot_general(a, b, (((1,), (0,)), ((), ())), preferred_element_type=F32)


def in_hbm(x):
    return pltpu.with_memory_space_constraint(x, pltpu.HBM)


def iota(shape, dim):
    return lax.broadcasted_iota(jnp.int32, shape, dim)


class Layout:
    def __init__(self, n_grp, n_ang, k_up, list_len):
        self.n_grp, self.n_ang = n_grp, n_ang
        self.n_dev = n_grp * n_ang
        self.own = k_up // self.n_dev
        self.pad = -(-self.own // 8) * 8
        self.list_len = list_len

    def first(self, dest):
        grp, ang = divmod(dest, self.n_ang)
        return (ang * self.n_grp + grp) * self.own


HALF = 64
NOTES = 48
CODE_BITS = 20
BIAS = 2048


def exponent(largest):
    return jnp.ceil(8.0 * jnp.log2(jnp.maximum(largest, 1e-30)))


def scale_of(eighths):
    return jnp.exp2(eighths * 0.125)


def pack(re, im, scale):
    def grid(x):
        return jnp.clip(jnp.round(x * (32767.0 / scale)), -32767.0, 32767.0).astype(jnp.int32)
    return jnp.bitwise_or(jnp.left_shift(grid(re), 16), jnp.bitwise_and(grid(im), 65535))


def unpack(words, scale):
    step = scale * (1.0 / 32767.0)
    re = jnp.right_shift(words, 16).astype(F32) * step
    im = jnp.right_shift(jnp.left_shift(words, 16), 16).astype(F32) * step
    return re, im


def note(word):
    return lax.shift_right_logical(word, CODE_BITS)


def piece(source, target, sems, dim, size):
    def at(i):
        index = (slice(None),) * dim + (pl.ds(pl.multiple_of(i * size, size), size),)
        return pltpu.make_async_copy(source.at[index], target.at[index], sems.at[i])
    return at


def forward_kernel(lay, ang_ref, cur_hbm, phase_hbm, src_hbm, kind_hbm, cols_hbm, rad_hbm, interp_hbm, out_ref, cos_ref,
                   sin_ref, cur_ref, phase_ref, src_ref, kind_ref, cols_ref, rad_ref, interp_ref, high_ref, low_ref,
                   par_ref, code_ref, small_sems, rad_sems, interp_sems):
    small = [
        pltpu.make_async_copy(source, target, small_sems.at[i])
        for i, (source, target) in enumerate([
            (cur_hbm, cur_ref), (phase_hbm, phase_ref), (src_hbm, src_ref), (kind_hbm, kind_ref),
            (cols_hbm, cols_ref)])
    ]
    for copy in small:
        copy.start()
    rad_piece = piece(rad_hbm, rad_ref, rad_sems, 1, TILE)
    interp_piece = piece(interp_hbm, interp_ref, interp_sems, 0, ROWS)
    n_rad, n_interp = rad_sems.shape[0], interp_sems.shape[0]
    for i in range(n_rad):
        rad_piece(i).start()
    interp_piece(0).start()
    for copy in small:
        copy.wait()
    count = cur_ref.shape[1]
    n_par = count // 8
    k_up, k_leaf = interp_ref.shape

    row = iota((count, count), 0)
    col = iota((count, count), 1)
    order = (col == (row % n_par) * 8 + row // n_par).astype(BF16)
    cur_re = dot_nn(order, cur_ref[0]).astype(BF16)
    cur_im = dot_nn(order, cur_ref[1]).astype(BF16)
    left = jnp.concatenate([cur_re, cur_im], axis=0)
    right = jnp.concatenate([-cur_im, cur_re], axis=0)
    cos_ref[...] = jnp.cos(phase_ref[...])
    sin_ref[...] = jnp.sin(phase_ref[...])

    src = src_ref[...]
    place = (jnp.left_shift(jnp.right_shift(src, 4), 3) + jnp.bitwise_and(src, 7)
             + jnp.bitwise_and(jnp.right_shift(src, 3), 1) * (lay.n_dev * n_par // 2))
    code_ref[:, 0:lay.list_len] = (place * 512 + kind_ref[...]).T
    codes = code_ref[pl.ds(pl.multiple_of(ang_ref[0] * n_par, n_par), n_par), 0:lay.list_len]
    n_ask = cols_ref.shape[1]
    asks = jnp.concatenate([cols_ref[...], jnp.zeros((1, 128 - n_ask), jnp.int32)], axis=1)
    asks = jnp.broadcast_to(asks, (8, 128)).T[:, 0:1]
    asks = [asks[b:b + n_par] for b in range(0, n_ask, n_par)]

    def radiate_tile(i, carry):
        rad_piece(i).wait()

        @pl.when(i + 1 < n_interp)
        def _():
            interp_piece(i + 1).start()

        at = pl.ds(pl.multiple_of(i * TILE, TILE), TILE)
        rr_high, rr_low = halves(rad_ref[0, at, :])
        ri_high, ri_low = halves(rad_ref[1, at, :])
        radiated = (dot_nt(left, rr_high) + dot_nt(left, rr_low)
                    + dot_nt(right, ri_high) + dot_nt(right, ri_low))
        high, low = halves(radiated)
        high_ref[:, at] = high
        low_ref[:, at] = low
        return carry

    lax.fori_loop(0, n_rad, radiate_tile, 0)

    def interp_tile(i, carry):
        interp_piece(i).wait()

        @pl.when(i + 1 + n_rad < n_interp)
        def _():
            interp_piece(i + 1 + n_rad).start()

        at = pl.ds(pl.multiple_of(i * ROWS, ROWS), ROWS)
        in_high, in_low = halves(interp_ref[at, :])
        children = (dot_nt(high_ref[...], in_high) + dot_nt(high_ref[...], in_low)
                    + dot_nt(low_ref[...], in_high))
        re_sum = im_sum = None
        for t in range(8):
            c = cos_ref[t:t + 1, at]
            s = sin_ref[t:t + 1, at]
            re = children[t * n_par:(t + 1) * n_par]
            im = children[count + t * n_par:count + (t + 1) * n_par]
            re_t = c * re - s * im
            im_t = c * im + s * re
            re_sum = re_t if t == 0 else re_sum + re_t
            im_sum = im_t if t == 0 else im_sum + im_t
        par_ref[0, :, at] = re_sum
        par_ref[1, :, at] = im_sum
        return carry

    lax.fori_loop(0, n_interp, interp_tile, 0)

    largest = jnp.max(jnp.maximum(jnp.abs(par_ref[0]), jnp.abs(par_ref[1])), axis=1, keepdims=True)
    eighths = exponent(largest)
    words = pack(par_ref[0], par_ref[1], scale_of(eighths))
    notes = [eighths.astype(jnp.int32) + BIAS] + asks
    notes.append(jnp.zeros((n_par, lay.list_len - len(notes)), jnp.int32))
    notes = codes + jnp.left_shift(jnp.concatenate(notes, axis=1), CODE_BITS)
    gap = [jnp.zeros((8, NOTES - lay.own), jnp.int32)] if lay.own < NOTES else []
    for dest in range(lay.n_dev):
        at = slice(lay.first(dest), lay.first(dest) + lay.own)
        out_ref[dest] = jnp.concatenate(
            [words[0:8, at], *gap, notes[0:8], words[8:16, at], *gap, notes[8:16]], axis=1)


def forward(lay, ang, current, radiate, interp, phase, sources, types, cols):
    count = current.shape[1]
    k_up, k_leaf = interp.shape
    n_par = count // 8
    return pl.pallas_call(
        functools.partial(forward_kernel, lay),
        in_specs=[SMEM] + [HBM] * 7,
        out_specs=[VMEM] * 3,
        out_shape=[
            jax.ShapeDtypeStruct((lay.n_dev, 8, 128), jnp.int32),
            jax.ShapeDtypeStruct(phase.shape, F32),
            jax.ShapeDtypeStruct(phase.shape, F32),
        ],
        scratch_shapes=[
            pltpu.VMEM(current.shape, BF16),
            pltpu.VMEM(phase.shape, F32),
            pltpu.VMEM(sources.shape[::-1], jnp.int32),
            pltpu.VMEM(types.shape[::-1], jnp.int32),
            pltpu.VMEM(cols.shape, jnp.int32),
            pltpu.VMEM(radiate.shape, F32),
            pltpu.VMEM(interp.shape, F32),
            pltpu.VMEM((2 * count, k_leaf), BF16),
            pltpu.VMEM((2 * count, k_leaf), BF16),
            pltpu.VMEM((2, n_par, k_up), F32),
            pltpu.VMEM((sources.shape[0], 128), jnp.int32),
            pltpu.SemaphoreType.DMA((5,)),
            pltpu.SemaphoreType.DMA((k_leaf // TILE,)),
            pltpu.SemaphoreType.DMA((k_up // ROWS,)),
        ],
        compiler_params=pltpu.CompilerParams(vmem_limit_bytes=VMEM_LIMIT),
        cost_estimate=pl.CostEstimate(flops=3 * 10**9, bytes_accessed=9 * 10**6, transcendentals=0),
        name="forward",
    )(ang, *map(in_hbm, (current, phase, sources.T, types.T, cols, radiate, interp)))


def translate_kernel(lay, got_ref, table_ref, out_ref, x_ref, t_ref, acc_ref):
    n_par = 2 * got_ref.shape[0]
    side = n_par // 2
    span = 2 * lay.pad
    n_pad = table_ref.shape[1]
    got = got_ref[...].T
    codes = []
    for h in range(2):
        words = got[HALF * h:HALF * h + lay.pad]
        codes.append(got[HALF * h + NOTES:HALF * h + NOTES + lay.list_len])
        scale = scale_of((note(codes[h][0:1]) - BIAS).astype(F32))
        for part, value in enumerate(unpack(words, scale)):
            high, low = halves(value)
            at = lay.pad * part
            x_ref[at:at + lay.pad, side * h:side * h + side] = high
            x_ref[span + at:span + at + lay.pad, side * h:side * h + side] = low
    codes = jnp.bitwise_and(jnp.concatenate(codes, axis=1), (1 << CODE_BITS) - 1)
    high, low = halves(table_ref[...])
    t_ref[0:span] = high
    t_ref[span:2 * span] = low
    width = min(512, n_par)
    rows_src = iota((n_par, width), 0)
    rows_kind = iota((n_pad, width), 0)
    for p in range(0, n_par, width):
        at = slice(p, p + width)
        re_sum = im_sum = 0.0
        for m in range(lay.list_len):
            code = codes[m:m + 1, at]
            source = jnp.right_shift(code, 9)
            kind = jnp.bitwise_and(code, 511)
            pick = (rows_src == source).astype(BF16)
            both = dot_nn(x_ref[...], pick)
            chosen = both[0:span] + both[span:2 * span]
            pick = (rows_kind == kind).astype(BF16)
            both = dot_nn(t_ref[...], pick)
            factor = both[0:span] + both[span:2 * span]
            fr, fi = factor[0:lay.pad], factor[lay.pad:span]
            cr, ci = chosen[0:lay.pad], chosen[lay.pad:span]
            re_sum = re_sum + (fr * cr - fi * ci)
            im_sum = im_sum + (fr * ci + fi * cr)
        largest = jnp.maximum(jnp.max(jnp.abs(re_sum), axis=0, keepdims=True),
                              jnp.max(jnp.abs(im_sum), axis=0, keepdims=True))
        eighths = exponent(largest)
        acc_ref[0:lay.pad, at] = pack(re_sum, im_sum, scale_of(eighths))
        acc_ref[NOTES:NOTES + 8, at] = jnp.broadcast_to(eighths, (8, width)).astype(jnp.int32)
    for h in range(2):
        out_ref[:, HALF * h:HALF * h + HALF] = acc_ref[:, side * h:side * h + side].T


def translate_far(lay, got, table):
    n_par = 2 * got.shape[0]
    span = 2 * lay.pad
    return pl.pallas_call(
        functools.partial(translate_kernel, lay),
        in_specs=[VMEM] * 2,
        out_specs=VMEM,
        out_shape=jax.ShapeDtypeStruct(got.shape, jnp.int32),
        scratch_shapes=[
            pltpu.VMEM((2 * span, n_par), BF16),
            pltpu.VMEM((2 * span, table.shape[1]), BF16),
            pltpu.VMEM((HALF, n_par), jnp.int32),
        ],
        compiler_params=pltpu.CompilerParams(vmem_limit_bytes=VMEM_LIMIT),
        cost_estimate=pl.CostEstimate(flops=2 * 10**9, bytes_accessed=10**6, transcendentals=0),
        name="translate_far",
    )(got, table)


def backward_kernel(lay, got_ref, cos_ref, sin_ref, near_ref, interp_hbm, rec_hbm, out_ref,
                    interp_ref, rec_ref, inc_ref, high_ref, low_ref, leaf_ref, interp_sems, rec_sems):
    interp_piece = piece(interp_hbm, interp_ref, interp_sems, 0, ROWS)
    rec_piece = piece(rec_hbm, rec_ref, rec_sems, 1, TILE)
    n_interp, n_rec = interp_sems.shape[0], rec_sems.shape[0]
    order = [(interp_piece, i) for i in range(n_interp)] + [(rec_piece, i) for i in range(n_rec)]
    for fetch, i in order[:3]:
        fetch(i).start()
    count = near_ref.shape[1]
    n_par = count // 8

    for dest in range(lay.n_dev):
        words = got_ref[dest]
        j = lay.first(dest)
        for h in range(2):
            eighths = words[:, HALF * h + NOTES:HALF * h + NOTES + 1].astype(F32)
            values = unpack(words[:, HALF * h:HALF * h + lay.own], scale_of(eighths))
            for part in range(2):
                inc_ref[part, 8 * h:8 * h + 8, j:j + lay.own] = values[part]
    c = cos_ref[...]
    s = sin_ref[...]
    for p in range(0, n_par, 2):
        res, ims = [], []
        for q in (p, p + 1):
            re = inc_ref[0, q:q + 1, :]
            im = inc_ref[1, q:q + 1, :]
            res.append(c * re + s * im)
            ims.append(c * im - s * re)
        high, low = halves(jnp.concatenate(res, axis=0))
        high_ref[8 * p:8 * p + 16] = high
        low_ref[8 * p:8 * p + 16] = low
        high, low = halves(jnp.concatenate(ims, axis=0))
        high_ref[count + 8 * p:count + 8 * p + 16] = high
        low_ref[count + 8 * p:count + 8 * p + 16] = low

    leaf_ref[...] = jnp.zeros_like(leaf_ref)

    def leaf_tile(i, carry):
        interp_piece(i).wait()

        for k, (fetch, which) in enumerate(order[3:]):
            @pl.when(i == min(k, n_interp - 1))
            def _():
                fetch(which).start()

        at = pl.ds(pl.multiple_of(i * ROWS, ROWS), ROWS)
        in_high, in_low = halves(interp_ref[at, :])
        leaf_ref[...] += (dot_nn(high_ref[:, at], in_high) + dot_nn(high_ref[:, at], in_low)
                          + dot_nn(low_ref[:, at], in_high))
        return carry

    lax.fori_loop(0, n_interp, leaf_tile, 0)
    for i in range(n_rec):
        rec_piece(i).wait()
    leaf_high, leaf_low = halves(leaf_ref[...])
    by = []
    for part in range(2):
        rec_high, rec_low = halves(rec_ref[part])
        by.append(dot_nn(leaf_high, rec_high) + dot_nn(leaf_high, rec_low) + dot_nn(leaf_low, rec_high))
    re_sum = near_ref[0] + (by[0][0:count] - by[1][count:2 * count])
    im_sum = near_ref[1] + (by[1][0:count] + by[0][count:2 * count])
    out_ref[0] = re_sum
    out_ref[1] = im_sum


def backward(lay, got, interp, receive, cosine, sine, near):
    count = near.shape[1]
    n_par = count // 8
    k_up, k_leaf = interp.shape
    unk = receive.shape[2]
    return pl.pallas_call(
        functools.partial(backward_kernel, lay),
        in_specs=[VMEM] * 4 + [HBM] * 2,
        out_specs=VMEM,
        out_shape=jax.ShapeDtypeStruct((2, count, unk), F32),
        scratch_shapes=[
            pltpu.VMEM(interp.shape, F32),
            pltpu.VMEM(receive.shape, F32),
            pltpu.VMEM((2, n_par, k_up), F32),
            pltpu.VMEM((2 * count, k_up), BF16),
            pltpu.VMEM((2 * count, k_up), BF16),
            pltpu.VMEM((2 * count, k_leaf), F32),
            pltpu.SemaphoreType.DMA((k_up // ROWS,)),
            pltpu.SemaphoreType.DMA((k_leaf // TILE,)),
        ],
        compiler_params=pltpu.CompilerParams(vmem_limit_bytes=VMEM_LIMIT),
        cost_estimate=pl.CostEstimate(flops=3 * 10**9, bytes_accessed=9 * 10**6, transcendentals=0),
        name="backward",
    )(pltpu.with_memory_space_constraint(got, pltpu.VMEM), cosine, sine, near, in_hbm(interp), in_hbm(receive))


def pick_kernel(lay, n_block, me_ref, got_ref, cur_ref, *out_refs):
    count = cur_ref.shape[1]
    first = me_ref[0]
    ang = me_ref[1]
    for mask, out_ref in enumerate(out_refs):
        dest = first + jnp.bitwise_xor(ang, mask)
        notes = note(got_ref[dest])
        marks = []
        for field in range(1, 1 + -(-n_block // 16)):
            for h in range(2):
                lane = HALF * h + NOTES + field
                marks.append((iota((8, count), 1) == notes[:, lane:lane + 1] - ang * count).astype(F32))
        mark = jnp.concatenate(marks, axis=0).astype(BF16)
        both = [dot_nn(mark, cur_ref[part])[0:n_block] for part in range(2)]
        out_ref[...] = jnp.concatenate(both, axis=0).astype(BF16)


def pick_columns(lay, n_block, me, got, current):
    unk = current.shape[2]
    one = jax.ShapeDtypeStruct((2 * n_block, unk), BF16)
    return pl.pallas_call(
        functools.partial(pick_kernel, lay, n_block),
        in_specs=[SMEM, VMEM, VMEM],
        out_specs=[VMEM] * lay.n_ang,
        out_shape=[one] * lay.n_ang,
        compiler_params=pltpu.CompilerParams(vmem_limit_bytes=VMEM_LIMIT),
        cost_estimate=pl.CostEstimate(flops=10**8, bytes_accessed=10**6, transcendentals=0),
        name="pick_columns",
    )(me, got, current)


def swap(picked, n_ang):
    first = 1
    kept = [mask for mask in range(n_ang) if not mask & first]
    sent = jnp.stack([picked[mask ^ first] for mask in kept])
    got = lax.ppermute(sent, "ang", [(i, i ^ first) for i in range(n_ang)])
    return {mask: picked[mask] + got[k] for k, mask in enumerate(kept)}


def answers(half, n_ang):
    masks = sorted(half)
    order = [masks[k ^ (k >> 1)] for k in range(1, len(masks))]
    return [half[0]] + [lax.ppermute(half[mask], "ang", [(i, i ^ mask) for i in range(n_ang)]) for mask in order]


def near_kernel(n_term, *refs):
    rows_ref, terms, (blocks_hbm, out_ref, blocks_ref, wide_ref, own_ref, sems) = (
        refs[0], refs[1:1 + n_term], refs[1 + n_term:])
    n_block, _, unk, _ = blocks_ref.shape
    here = n_block // sems.shape[0]

    block_piece = piece(blocks_hbm, blocks_ref, sems, 0, here)
    n_piece = sems.shape[0]
    for i in range(3):
        block_piece(i).start()
    total = terms[0][...].astype(F32)
    for term in terms[1:]:
        total = total + term[...].astype(F32)
    gap = jnp.zeros((64 - n_block, unk), F32)
    wide_ref[...] = jnp.concatenate([total[0:n_block], gap, total[n_block:], gap], axis=0).astype(BF16)
    lane = iota((2 * unk, 128), 1) % 64
    own_ref[...] = jnp.zeros_like(own_ref)

    def some_blocks(i, carry):
        block_piece(i).wait()

        @pl.when(i + 3 < n_piece)
        def _():
            block_piece(i + 3).start()

        rows = blocks_ref[pl.ds(i * here, here)].reshape(here * 2 * unk, unk)
        products = dot_nt(rows, wide_ref[...])
        own = own_ref[...]
        for k in range(here):
            own = jnp.where(lane == i * here + k, products[2 * unk * k:2 * unk * (k + 1)], own)
        own_ref[...] = own
        return carry

    lax.fori_loop(0, n_piece, some_blocks, 0)

    by_block = own_ref[...].T
    by_re, by_im = by_block[:, 0:unk], by_block[:, unk:2 * unk]
    re = by_re[0:n_block] - by_im[64:64 + n_block]
    im = by_re[64:64 + n_block] + by_im[0:n_block]
    count = out_ref.shape[1]
    mark = (iota((count, n_block), 0) == rows_ref[...]).astype(BF16)
    for part, value in ((0, re), (1, im)):
        high, low = halves(value)
        out_ref[part] = dot_nn(mark, high) + dot_nn(mark, low)


def near_field(rows, terms, blocks, count):
    n_block, _, unk, _ = blocks.shape
    here = 8
    return pl.pallas_call(
        functools.partial(near_kernel, len(terms)),
        in_specs=[VMEM] * (1 + len(terms)) + [HBM],
        out_specs=VMEM,
        out_shape=jax.ShapeDtypeStruct((2, count, unk), F32),
        scratch_shapes=[
            pltpu.VMEM(blocks.shape, BF16),
            pltpu.VMEM((128, unk), BF16),
            pltpu.VMEM((2 * unk, 128), F32),
            pltpu.SemaphoreType.DMA((n_block // here,)),
        ],
        compiler_params=pltpu.CompilerParams(vmem_limit_bytes=VMEM_LIMIT),
        cost_estimate=pl.CostEstimate(flops=2 * 10**10, bytes_accessed=12 * 10**6, transcendentals=0),
        name="near_field",
    )(rows, *terms, in_hbm(blocks))


def on_device(n_grp, n_ang, current, near_blocks, near_rows, near_cols, radiate, receive, interp,
              shift_phase, translate, far_sources, far_types):
    count, unk = current.shape[1:]
    n_par = count // 8
    n_block = near_blocks.shape[0]
    k_up = interp.shape[0]
    n_kind = translate.shape[1]
    lay = Layout(n_grp, n_ang, k_up, far_sources.shape[1])
    grp = lax.axis_index("grp")
    ang = lax.axis_index("ang")
    axes = ("grp", "ang")

    message, cosine, sine = forward(
        lay, ang[None], current, radiate, interp, shift_phase, far_sources, far_types, near_cols[None])
    got = lax.all_to_all(message, axes, 0, 0)
    half = swap(pick_columns(lay, n_block, jnp.stack([grp * n_ang, ang]), got, current), n_ang)

    table = lax.dynamic_slice_in_dim(translate, grp * lay.own, lay.own, 2)
    kind_pad = -(-n_kind // 128) * 128
    table = jnp.pad(table, ((0, 0), (0, kind_pad - n_kind), (0, lay.pad - lay.own)))
    table = jnp.transpose(table, (0, 2, 1)).reshape(2 * lay.pad, kind_pad)

    incoming = translate_far(lay, got.reshape(lay.n_dev * 8, 128), table)
    incoming, half = lax.optimization_barrier((incoming, half))
    near = near_field(near_rows[None], answers(half, n_ang), near_blocks, count)
    returned = lax.all_to_all(incoming.reshape(lay.n_dev, 8, 128), axes, 0, 0)

    return backward(lay, returned, interp, receive, cosine, sine, near)


def solution(mesh):
    both = ("grp", "ang")
    in_specs = (
        P(None, both, None),
        P(both, None, None, None),
        P(both),
        P(both),
        P(),
        P(),
        P(),
        P(),
        P(None, None, "ang"),
        P("grp", None),
        P("grp", None),
    )
    run = functools.partial(on_device, mesh.shape["grp"], mesh.shape["ang"])
    return jax.shard_map(run, mesh=mesh, in_specs=in_specs, out_specs=P(None, both, None), check_vma=False)
```

```python
import functools
import jax
import jax.numpy as jnp
from jax import lax
from jax.experimental import pallas as pl
from jax.experimental.pallas import tpu as pltpu
from jax.sharding import PartitionSpec as P

F32 = jnp.float32
BF16 = jnp.bfloat16
VMEM_LIMIT = 24 << 20
HBM = pl.BlockSpec(memory_space=pltpu.HBM)
VMEM = pl.BlockSpec(memory_space=pltpu.VMEM)
SMEM = pl.BlockSpec(memory_space=pltpu.SMEM)
TILE = 512
ROWS = 512


def halves(x):
    high = x.astype(BF16)
    return high, (x - high.astype(F32)).astype(BF16)


def dot_nt(a, b):
    return lax.dot_general(a, b, (((1,), (1,)), ((), ())), preferred_element_type=F32)


def dot_nn(a, b):
    return lax.dot_general(a, b, (((1,), (0,)), ((), ())), preferred_element_type=F32)


def in_hbm(x):
    return pltpu.with_memory_space_constraint(x, pltpu.HBM)


def iota(shape, dim):
    return lax.broadcasted_iota(jnp.int32, shape, dim)


class Layout:
    def __init__(self, n_grp, n_ang, k_up, list_len):
        self.n_grp, self.n_ang = n_grp, n_ang
        self.n_dev = n_grp * n_ang
        self.own = k_up // self.n_dev
        self.pad = -(-self.own // 8) * 8
        self.list_len = list_len

    def first(self, dest):
        grp, ang = divmod(dest, self.n_ang)
        return (ang * self.n_grp + grp) * self.own


HALF = 64
NOTES = 48
CODE_BITS = 20
BIAS = 2048


def exponent(largest):
    return jnp.ceil(8.0 * jnp.log2(jnp.maximum(largest, 1e-37)))


def scale_of(eighths):
    return jnp.exp2(eighths * 0.125)


def pack(re, im, scale):
    def grid(x):
        return jnp.clip(jnp.round(x * (1.0 / scale) * 32767.0), -32767.0, 32767.0).astype(jnp.int32)
    return jnp.bitwise_or(jnp.left_shift(grid(re), 16), jnp.bitwise_and(grid(im), 65535))


def unpack(words, scale):
    re = jnp.right_shift(words, 16).astype(F32) * (1.0 / 32767.0) * scale
    im = jnp.right_shift(jnp.left_shift(words, 16), 16).astype(F32) * (1.0 / 32767.0) * scale
    return re, im


def note(word):
    return lax.shift_right_logical(word, CODE_BITS)


def piece(source, target, sems, dim, size):
    def at(i):
        index = (slice(None),) * dim + (pl.ds(pl.multiple_of(i * size, size), size),)
        return pltpu.make_async_copy(source.at[index], target.at[index], sems.at[i])
    return at


def forward_kernel(lay, ang_ref, cur_hbm, phase_hbm, src_hbm, kind_hbm, cols_hbm, rad_hbm, interp_hbm, out_ref, cos_ref,
                   sin_ref, cur_ref, phase_ref, src_ref, kind_ref, cols_ref, rad_ref, interp_ref, high_ref, low_ref,
                   par_ref, code_ref, small_sems, rad_sems, interp_sems):
    small = [
        pltpu.make_async_copy(source, target, small_sems.at[i])
        for i, (source, target) in enumerate([
            (cur_hbm, cur_ref), (phase_hbm, phase_ref), (src_hbm, src_ref), (kind_hbm, kind_ref),
            (cols_hbm, cols_ref)])
    ]
    for copy in small:
        copy.start()
    rad_piece = piece(rad_hbm, rad_ref, rad_sems, 1, TILE)
    interp_piece = piece(interp_hbm, interp_ref, interp_sems, 0, ROWS)
    n_rad, n_interp = rad_sems.shape[0], interp_sems.shape[0]
    for i in range(n_rad):
        rad_piece(i).start()
    interp_piece(0).start()
    for copy in small:
        copy.wait()
    count = cur_ref.shape[1]
    n_par = count // 8
    k_up, k_leaf = interp_ref.shape

    row = iota((count, count), 0)
    col = iota((count, count), 1)
    order = (col == (row % n_par) * 8 + row // n_par).astype(BF16)
    cur_re = dot_nn(order, cur_ref[0]).astype(BF16)
    cur_im = dot_nn(order, cur_ref[1]).astype(BF16)
    left = jnp.concatenate([cur_re, cur_im], axis=0)
    right = jnp.concatenate([-cur_im, cur_re], axis=0)
    cos_ref[...] = jnp.cos(phase_ref[...])
    sin_ref[...] = jnp.sin(phase_ref[...])

    src = src_ref[...]
    place = (jnp.left_shift(jnp.right_shift(src, 4), 3) + jnp.bitwise_and(src, 7)
             + jnp.bitwise_and(jnp.right_shift(src, 3), 1) * (lay.n_dev * n_par // 2))
    code_ref[:, 0:lay.list_len] = (place * 512 + kind_ref[...]).T
    codes = code_ref[pl.ds(pl.multiple_of(ang_ref[0] * n_par, n_par), n_par), 0:lay.list_len]
    n_ask = cols_ref.shape[1]
    asks = jnp.concatenate([cols_ref[...], jnp.zeros((1, 128 - n_ask), jnp.int32)], axis=1)
    asks = jnp.broadcast_to(asks, (8, 128)).T[:, 0:1]
    asks = [asks[b:b + n_par] for b in range(0, n_ask, n_par)]

    def radiate_tile(i, carry):
        rad_piece(i).wait()

        @pl.when(i + 1 < n_interp)
        def _():
            interp_piece(i + 1).start()

        at = pl.ds(pl.multiple_of(i * TILE, TILE), TILE)
        rr_high, rr_low = halves(rad_ref[0, at, :])
        ri_high, ri_low = halves(rad_ref[1, at, :])
        radiated = (dot_nt(left, rr_high) + dot_nt(left, rr_low)
                    + dot_nt(right, ri_high) + dot_nt(right, ri_low))
        high, low = halves(radiated)
        high_ref[:, at] = high
        low_ref[:, at] = low
        return carry

    lax.fori_loop(0, n_rad, radiate_tile, 0)

    def interp_tile(i, carry):
        interp_piece(i).wait()

        @pl.when(i + 1 + n_rad < n_interp)
        def _():
            interp_piece(i + 1 + n_rad).start()

        at = pl.ds(pl.multiple_of(i * ROWS, ROWS), ROWS)
        in_high, in_low = halves(interp_ref[at, :])
        children = (dot_nt(high_ref[...], in_high) + dot_nt(high_ref[...], in_low)
                    + dot_nt(low_ref[...], in_high))
        re_sum = im_sum = None
        for t in range(8):
            c = cos_ref[t:t + 1, at]
            s = sin_ref[t:t + 1, at]
            re = children[t * n_par:(t + 1) * n_par]
            im = children[count + t * n_par:count + (t + 1) * n_par]
            re_t = c * re - s * im
            im_t = c * im + s * re
            re_sum = re_t if t == 0 else re_sum + re_t
            im_sum = im_t if t == 0 else im_sum + im_t
        par_ref[0, :, at] = re_sum
        par_ref[1, :, at] = im_sum
        return carry

    lax.fori_loop(0, n_interp, interp_tile, 0)

    largest = jnp.max(jnp.maximum(jnp.abs(par_ref[0]), jnp.abs(par_ref[1])), axis=1, keepdims=True)
    eighths = exponent(largest)
    words = pack(par_ref[0], par_ref[1], scale_of(eighths))
    notes = [eighths.astype(jnp.int32) + BIAS] + asks
    notes.append(jnp.zeros((n_par, lay.list_len - len(notes)), jnp.int32))
    notes = codes + jnp.left_shift(jnp.concatenate(notes, axis=1), CODE_BITS)
    gap = [jnp.zeros((8, NOTES - lay.own), jnp.int32)] if lay.own < NOTES else []
    for dest in range(lay.n_dev):
        at = slice(lay.first(dest), lay.first(dest) + lay.own)
        out_ref[dest] = jnp.concatenate(
            [words[0:8, at], *gap, notes[0:8], words[8:16, at], *gap, notes[8:16]], axis=1)


def forward(lay, ang, current, radiate, interp, phase, sources, types, cols):
    count = current.shape[1]
    k_up, k_leaf = interp.shape
    n_par = count // 8
    return pl.pallas_call(
        functools.partial(forward_kernel, lay),
        in_specs=[SMEM] + [HBM] * 7,
        out_specs=[VMEM] * 3,
        out_shape=[
            jax.ShapeDtypeStruct((lay.n_dev, 8, 128), jnp.int32),
            jax.ShapeDtypeStruct(phase.shape, F32),
            jax.ShapeDtypeStruct(phase.shape, F32),
        ],
        scratch_shapes=[
            pltpu.VMEM(current.shape, BF16),
            pltpu.VMEM(phase.shape, F32),
            pltpu.VMEM(sources.shape[::-1], jnp.int32),
            pltpu.VMEM(types.shape[::-1], jnp.int32),
            pltpu.VMEM(cols.shape, jnp.int32),
            pltpu.VMEM(radiate.shape, F32),
            pltpu.VMEM(interp.shape, F32),
            pltpu.VMEM((2 * count, k_leaf), BF16),
            pltpu.VMEM((2 * count, k_leaf), BF16),
            pltpu.VMEM((2, n_par, k_up), F32),
            pltpu.VMEM((sources.shape[0], 128), jnp.int32),
            pltpu.SemaphoreType.DMA((5,)),
            pltpu.SemaphoreType.DMA((k_leaf // TILE,)),
            pltpu.SemaphoreType.DMA((k_up // ROWS,)),
        ],
        compiler_params=pltpu.CompilerParams(vmem_limit_bytes=VMEM_LIMIT),
        cost_estimate=pl.CostEstimate(flops=3 * 10**9, bytes_accessed=9 * 10**6, transcendentals=0),
        name="forward",
    )(ang, *map(in_hbm, (current, phase, sources.T, types.T, cols, radiate, interp)))


def translate_kernel(lay, got_ref, table_ref, out_ref, x_ref, t_ref, acc_ref):
    n_par = 2 * got_ref.shape[0]
    side = n_par // 2
    span = 2 * lay.pad
    n_pad = table_ref.shape[1]
    got = got_ref[...].T
    codes = []
    for h in range(2):
        words = got[HALF * h:HALF * h + lay.pad]
        codes.append(got[HALF * h + NOTES:HALF * h + NOTES + lay.list_len])
        scale = scale_of((note(codes[h][0:1]) - BIAS).astype(F32))
        for part, value in enumerate(unpack(words, scale)):
            high, low = halves(value)
            at = lay.pad * part
            x_ref[at:at + lay.pad, side * h:side * h + side] = high
            x_ref[span + at:span + at + lay.pad, side * h:side * h + side] = low
    codes = jnp.bitwise_and(jnp.concatenate(codes, axis=1), (1 << CODE_BITS) - 1)
    high, low = halves(table_ref[...])
    t_ref[0:span] = high
    t_ref[span:2 * span] = low
    width = min(512, n_par)
    rows_src = iota((n_par, width), 0)
    rows_kind = iota((n_pad, width), 0)
    for p in range(0, n_par, width):
        at = slice(p, p + width)
        re_sum = im_sum = 0.0
        for m in range(lay.list_len):
            code = codes[m:m + 1, at]
            source = jnp.right_shift(code, 9)
            kind = jnp.bitwise_and(code, 511)
            pick = (rows_src == source).astype(BF16)
            both = dot_nn(x_ref[...], pick)
            chosen = both[0:span] + both[span:2 * span]
            pick = (rows_kind == kind).astype(BF16)
            both = dot_nn(t_ref[...], pick)
            factor = both[0:span] + both[span:2 * span]
            fr, fi = factor[0:lay.pad], factor[lay.pad:span]
            cr, ci = chosen[0:lay.pad], chosen[lay.pad:span]
            re_sum = re_sum + (fr * cr - fi * ci)
            im_sum = im_sum + (fr * ci + fi * cr)
        largest = jnp.maximum(jnp.max(jnp.abs(re_sum), axis=0, keepdims=True),
                              jnp.max(jnp.abs(im_sum), axis=0, keepdims=True))
        eighths = exponent(largest)
        acc_ref[0:lay.pad, at] = pack(re_sum, im_sum, scale_of(eighths))
        acc_ref[NOTES:NOTES + 8, at] = jnp.broadcast_to(eighths, (8, width)).astype(jnp.int32)
    for h in range(2):
        out_ref[:, HALF * h:HALF * h + HALF] = acc_ref[:, side * h:side * h + side].T


def translate_far(lay, got, table):
    n_par = 2 * got.shape[0]
    span = 2 * lay.pad
    return pl.pallas_call(
        functools.partial(translate_kernel, lay),
        in_specs=[VMEM] * 2,
        out_specs=VMEM,
        out_shape=jax.ShapeDtypeStruct(got.shape, jnp.int32),
        scratch_shapes=[
            pltpu.VMEM((2 * span, n_par), BF16),
            pltpu.VMEM((2 * span, table.shape[1]), BF16),
            pltpu.VMEM((HALF, n_par), jnp.int32),
        ],
        compiler_params=pltpu.CompilerParams(vmem_limit_bytes=VMEM_LIMIT),
        cost_estimate=pl.CostEstimate(flops=2 * 10**9, bytes_accessed=10**6, transcendentals=0),
        name="translate_far",
    )(got, table)


def backward_kernel(lay, got_ref, cos_ref, sin_ref, near_ref, interp_hbm, rec_hbm, out_ref,
                    interp_ref, rec_ref, inc_ref, high_ref, low_ref, leaf_ref, interp_sems, rec_sems):
    interp_piece = piece(interp_hbm, interp_ref, interp_sems, 0, ROWS)
    rec_piece = piece(rec_hbm, rec_ref, rec_sems, 1, TILE)
    n_interp, n_rec = interp_sems.shape[0], rec_sems.shape[0]
    order = [(interp_piece, i) for i in range(n_interp)] + [(rec_piece, i) for i in range(n_rec)]
    for fetch, i in order[:3]:
        fetch(i).start()
    count = near_ref.shape[1]
    n_par = count // 8

    for dest in range(lay.n_dev):
        words = got_ref[dest]
        j = lay.first(dest)
        for h in range(2):
            eighths = words[:, HALF * h + NOTES:HALF * h + NOTES + 1].astype(F32)
            values = unpack(words[:, HALF * h:HALF * h + lay.own], scale_of(eighths))
            for part in range(2):
                inc_ref[part, 8 * h:8 * h + 8, j:j + lay.own] = values[part]
    c = cos_ref[...]
    s = sin_ref[...]
    for p in range(0, n_par, 2):
        res, ims = [], []
        for q in (p, p + 1):
            re = inc_ref[0, q:q + 1, :]
            im = inc_ref[1, q:q + 1, :]
            res.append(c * re + s * im)
            ims.append(c * im - s * re)
        high, low = halves(jnp.concatenate(res, axis=0))
        high_ref[8 * p:8 * p + 16] = high
        low_ref[8 * p:8 * p + 16] = low
        high, low = halves(jnp.concatenate(ims, axis=0))
        high_ref[count + 8 * p:count + 8 * p + 16] = high
        low_ref[count + 8 * p:count + 8 * p + 16] = low

    leaf_ref[...] = jnp.zeros_like(leaf_ref)

    def leaf_tile(i, carry):
        interp_piece(i).wait()

        for k, (fetch, which) in enumerate(order[3:]):
            @pl.when(i == min(k, n_interp - 1))
            def _():
                fetch(which).start()

        at = pl.ds(pl.multiple_of(i * ROWS, ROWS), ROWS)
        in_high, in_low = halves(interp_ref[at, :])
        leaf_ref[...] += (dot_nn(high_ref[:, at], in_high) + dot_nn(high_ref[:, at], in_low)
                          + dot_nn(low_ref[:, at], in_high))
        return carry

    lax.fori_loop(0, n_interp, leaf_tile, 0)
    for i in range(n_rec):
        rec_piece(i).wait()
    leaf_high, leaf_low = halves(leaf_ref[...])
    by = []
    for part in range(2):
        rec_high, rec_low = halves(rec_ref[part])
        by.append(dot_nn(leaf_high, rec_high) + dot_nn(leaf_high, rec_low) + dot_nn(leaf_low, rec_high))
    re_sum = near_ref[0] + (by[0][0:count] - by[1][count:2 * count])
    im_sum = near_ref[1] + (by[1][0:count] + by[0][count:2 * count])
    out_ref[0] = re_sum
    out_ref[1] = im_sum


def backward(lay, got, interp, receive, cosine, sine, near):
    count = near.shape[1]
    n_par = count // 8
    k_up, k_leaf = interp.shape
    unk = receive.shape[2]
    return pl.pallas_call(
        functools.partial(backward_kernel, lay),
        in_specs=[VMEM] * 4 + [HBM] * 2,
        out_specs=VMEM,
        out_shape=jax.ShapeDtypeStruct((2, count, unk), F32),
        scratch_shapes=[
            pltpu.VMEM(interp.shape, F32),
            pltpu.VMEM(receive.shape, F32),
            pltpu.VMEM((2, n_par, k_up), F32),
            pltpu.VMEM((2 * count, k_up), BF16),
            pltpu.VMEM((2 * count, k_up), BF16),
            pltpu.VMEM((2 * count, k_leaf), F32),
            pltpu.SemaphoreType.DMA((k_up // ROWS,)),
            pltpu.SemaphoreType.DMA((k_leaf // TILE,)),
        ],
        compiler_params=pltpu.CompilerParams(vmem_limit_bytes=VMEM_LIMIT),
        cost_estimate=pl.CostEstimate(flops=3 * 10**9, bytes_accessed=9 * 10**6, transcendentals=0),
        name="backward",
    )(pltpu.with_memory_space_constraint(got, pltpu.VMEM), cosine, sine, near, in_hbm(interp), in_hbm(receive))


def pick_kernel(lay, n_block, me_ref, got_ref, cur_ref, *out_refs):
    count = cur_ref.shape[1]
    first = me_ref[0]
    ang = me_ref[1]
    for mask, out_ref in enumerate(out_refs):
        dest = first + jnp.bitwise_xor(ang, mask)
        notes = note(got_ref[dest])
        marks = []
        for field in range(1, 1 + -(-n_block // 16)):
            for h in range(2):
                lane = HALF * h + NOTES + field
                marks.append((iota((8, count), 1) == notes[:, lane:lane + 1] - ang * count).astype(F32))
        mark = jnp.concatenate(marks, axis=0).astype(BF16)
        both = [dot_nn(mark, cur_ref[part])[0:n_block] for part in range(2)]
        out_ref[...] = jnp.concatenate(both, axis=0).astype(BF16)


def pick_columns(lay, n_block, me, got, current):
    unk = current.shape[2]
    one = jax.ShapeDtypeStruct((2 * n_block, unk), BF16)
    return pl.pallas_call(
        functools.partial(pick_kernel, lay, n_block),
        in_specs=[SMEM, VMEM, VMEM],
        out_specs=[VMEM] * lay.n_ang,
        out_shape=[one] * lay.n_ang,
        compiler_params=pltpu.CompilerParams(vmem_limit_bytes=VMEM_LIMIT),
        cost_estimate=pl.CostEstimate(flops=10**8, bytes_accessed=10**6, transcendentals=0),
        name="pick_columns",
    )(me, got, current)


def swap(picked, n_ang):
    first = 1
    kept = [mask for mask in range(n_ang) if not mask & first]
    sent = jnp.stack([picked[mask ^ first] for mask in kept])
    got = lax.ppermute(sent, "ang", [(i, i ^ first) for i in range(n_ang)])
    return {mask: picked[mask] + got[k] for k, mask in enumerate(kept)}


def answers(half, n_ang):
    masks = sorted(half)
    order = [masks[k ^ (k >> 1)] for k in range(1, len(masks))]
    return [half[0]] + [lax.ppermute(half[mask], "ang", [(i, i ^ mask) for i in range(n_ang)]) for mask in order]


def near_kernel(n_term, *refs):
    rows_ref, terms, (blocks_hbm, out_ref, blocks_ref, wide_ref, own_ref, sems) = (
        refs[0], refs[1:1 + n_term], refs[1 + n_term:])
    n_block, _, unk, _ = blocks_ref.shape
    here = n_block // sems.shape[0]

    block_piece = piece(blocks_hbm, blocks_ref, sems, 0, here)
    n_piece = sems.shape[0]
    for i in range(3):
        block_piece(i).start()
    total = terms[0][...].astype(F32)
    for term in terms[1:]:
        total = total + term[...].astype(F32)
    gap = jnp.zeros((64 - n_block, unk), F32)
    wide_ref[...] = jnp.concatenate([total[0:n_block], gap, total[n_block:], gap], axis=0).astype(BF16)
    lane = iota((2 * unk, 128), 1) % 64
    own_ref[...] = jnp.zeros_like(own_ref)

    def some_blocks(i, carry):
        block_piece(i).wait()

        @pl.when(i + 3 < n_piece)
        def _():
            block_piece(i + 3).start()

        rows = blocks_ref[pl.ds(i * here, here)].reshape(here * 2 * unk, unk)
        products = dot_nt(rows, wide_ref[...])
        own = own_ref[...]
        for k in range(here):
            own = jnp.where(lane == i * here + k, products[2 * unk * k:2 * unk * (k + 1)], own)
        own_ref[...] = own
        return carry

    lax.fori_loop(0, n_piece, some_blocks, 0)

    by_block = own_ref[...].T
    by_re, by_im = by_block[:, 0:unk], by_block[:, unk:2 * unk]
    re = by_re[0:n_block] - by_im[64:64 + n_block]
    im = by_re[64:64 + n_block] + by_im[0:n_block]
    count = out_ref.shape[1]
    mark = (iota((count, n_block), 0) == rows_ref[...]).astype(BF16)
    for part, value in ((0, re), (1, im)):
        high, low = halves(value)
        out_ref[part] = dot_nn(mark, high) + dot_nn(mark, low)


def near_field(rows, terms, blocks, count):
    n_block, _, unk, _ = blocks.shape
    here = 8
    return pl.pallas_call(
        functools.partial(near_kernel, len(terms)),
        in_specs=[VMEM] * (1 + len(terms)) + [HBM],
        out_specs=VMEM,
        out_shape=jax.ShapeDtypeStruct((2, count, unk), F32),
        scratch_shapes=[
            pltpu.VMEM(blocks.shape, BF16),
            pltpu.VMEM((128, unk), BF16),
            pltpu.VMEM((2 * unk, 128), F32),
            pltpu.SemaphoreType.DMA((n_block // here,)),
        ],
        compiler_params=pltpu.CompilerParams(vmem_limit_bytes=VMEM_LIMIT),
        cost_estimate=pl.CostEstimate(flops=2 * 10**10, bytes_accessed=12 * 10**6, transcendentals=0),
        name="near_field",
    )(rows, *terms, in_hbm(blocks))


def on_device(n_grp, n_ang, current, near_blocks, near_rows, near_cols, radiate, receive, interp,
              shift_phase, translate, far_sources, far_types):
    count, unk = current.shape[1:]
    n_par = count // 8
    n_block = near_blocks.shape[0]
    k_up = interp.shape[0]
    n_kind = translate.shape[1]
    lay = Layout(n_grp, n_ang, k_up, far_sources.shape[1])
    grp = lax.axis_index("grp")
    ang = lax.axis_index("ang")
    axes = ("grp", "ang")

    message, cosine, sine = forward(
        lay, ang[None], current, radiate, interp, shift_phase, far_sources, far_types, near_cols[None])
    got = lax.all_to_all(message, axes, 0, 0)
    half = swap(pick_columns(lay, n_block, jnp.stack([grp * n_ang, ang]), got, current), n_ang)

    table = lax.dynamic_slice_in_dim(translate, grp * lay.own, lay.own, 2)
    kind_pad = -(-n_kind // 128) * 128
    table = jnp.pad(table, ((0, 0), (0, kind_pad - n_kind), (0, lay.pad - lay.own)))
    table = jnp.transpose(table, (0, 2, 1)).reshape(2 * lay.pad, kind_pad)

    incoming = translate_far(lay, got.reshape(lay.n_dev * 8, 128), table)
    incoming, half = lax.optimization_barrier((incoming, half))
    near = near_field(near_rows[None], answers(half, n_ang), near_blocks, count)
    returned = lax.all_to_all(incoming.reshape(lay.n_dev, 8, 128), axes, 0, 0)

    return backward(lay, returned, interp, receive, cosine, sine, near)


def solution(mesh):
    both = ("grp", "ang")
    in_specs = (
        P(None, both, None),
        P(both, None, None, None),
        P(both),
        P(both),
        P(),
        P(),
        P(),
        P(),
        P(None, None, "ang"),
        P("grp", None),
        P("grp", None),
    )
    run = functools.partial(on_device, mesh.shape["grp"], mesh.shape["ang"])
    return jax.shard_map(run, mesh=mesh, in_specs=in_specs, out_specs=P(None, both, None), check_vma=False)
```
